256 devices in a mesh: dp: 8 (over x, z_lo), tensor: 32 (over y, z_hi, core).
Axes of the slice: x: 4, y: 4, z: 8 (z_hi: 4, z_lo: 2; z = z_hi * 2 + z_lo), core: 2. Of those that a mesh axis runs over, the one named last changes fastest.
Arguments:
- normed: bfloat16 [8, 256, 16384], P('dp', None, 'tensor'), may hold values from -24 to 24
- queries: bfloat16 [8, 256, 8192], P('dp', None, 'tensor'), may hold values from -17 to 17
- keys: bfloat16 [8, 256, 512], P('dp', None, 'tensor'), may hold values from -5 to 5
- values: bfloat16 [8, 256, 512], P('dp', None, 'tensor'), may hold values from -5 to 5
- context_grad: bfloat16 [8, 256, 8192], P('dp', None, 'tensor'), may hold values from -5 to 5
- segments: int32 [8, 256], P('dp'), may hold values from 0 to 3, as said below
- w_query: bfloat16 [16384, 8192], P('tensor'), may hold values from -0.046875 to 0.046875
- w_key: bfloat16 [16384, 512], P('tensor'), may hold values from -0.046875 to 0.046875
- w_value: bfloat16 [16384, 512], P('tensor'), may hold values from -0.046875 to 0.046875
- adapter_down: bfloat16 [3, 16, 16384], P(None, None, 'tensor'), may hold values from -0.046875 to 0.046875
- up_query: bfloat16 [16, 8192], P(None, 'tensor'), may hold values from -0.59765625 to 0.59765625
- up_keyvalue: bfloat16 [2, 16, 512], P(None, None, 'tensor'), may hold values from -0.1796875 to 0.1796875
- accum_down: float32 [3, 16, 16384], P(None, 'dp', 'tensor'), may hold values from -1.2 to 1.2
- accum_query: float32 [16, 8192], P('dp', 'tensor'), may hold values from -0.3 to 0.3
- accum_keyvalue: float32 [2, 16, 512], P(None, 'dp', 'tensor'), may hold values from -0.6 to 0.6
Outputs:
- input_grad: bfloat16 [8, 256, 16384], P('dp', None, 'tensor')
- accum_down_new: float32 [3, 16, 16384], P(None, 'dp', 'tensor')
- accum_query_new: float32 [16, 8192], P('dp', 'tensor')
- accum_keyvalue_new: float32 [2, 16, 512], P(None, 'dp', 'tensor')
The draws below stay inside these ranges and needn't reach their ends.
Inputs may be any that keep to these rules, and one draw needn't show every extreme that they name: `segments`: within each sequence the ids begin at 0, never fall, and the last token's id is 3.
All inputs are finite; a program needn't handle non-finite values.
Results may differ from the reference program's by a relative error of at most 0.0059.
Values may be sent and summed in bfloat16 or wider, within the bound.
A program may use at most 64 MiB of HBM per device.

```python
import math
import jax
import jax.numpy as jnp
from jax import lax

D = 16384
QH = 64
KVH = 4
HD = 128
RANK = 16
SEQ = 256
SEQS = 8
QD = 8192
KVD = 512


def doc_starts(key):
    base = jax.random.fold_in(key, 101)
    draws = jax.random.randint(base, (SEQS, SEQ), 0, SEQ)
    places = jnp.arange(SEQ)[None, :]
    forced = (places == 0) | (places == SEQ // 4) | (places == SEQ // 2) | (places == 3 * SEQ // 4)
    return jnp.where((draws < 4) | forced, 1, 0).astype(jnp.int32)


def draw_segments(key, part):
    starts = doc_starts(key)
    return jnp.minimum(jnp.cumsum(starts, axis=1) - 1, 3).astype(jnp.int32)


def draw_keys(key, part):
    key = jax.random.fold_in(key, 11)
    result = jnp.clip(jax.random.normal(key, (SEQS, SEQ, KVD)), -4.0, 4.0)
    return result.astype(jnp.bfloat16)


def draw_queries(key, part):
    key = jax.random.fold_in(key, 12)
    result = jnp.clip(jax.random.normal(key, (SEQS, SEQ, QD)), -4.0, 4.0)
    return result.astype(jnp.bfloat16)


def draw_normed(key, part):
    key = jax.random.fold_in(key, 14)
    noise_key = jax.random.fold_in(key, 0)
    column_key = jax.random.fold_in(key, 2)
    common_key = jax.random.fold_in(key, 3)
    ramp = jnp.exp(math.log(3.0) * (jnp.arange(D, dtype=jnp.float32) / D - 0.5))
    columns = ramp * jnp.exp(jax.random.uniform(column_key, (D,), minval=math.log(0.5), maxval=math.log(2.0)))
    common = jnp.clip(jax.random.normal(common_key, (SEQS, 1, D)), -3.0, 3.0)
    base = jnp.clip(jax.random.normal(noise_key, (SEQS, SEQ, D)), -4.0, 4.0)
    result = (base + 0.8 * common) * columns
    return jnp.clip(result, -24.0, 24.0).astype(jnp.bfloat16)


def draw_context_grad(key, part):
    key = jax.random.fold_in(key, 15)
    noise_key, common_key = jax.random.split(key, 2)
    common = jnp.clip(jax.random.normal(common_key, (SEQS, 1, QD)), -3.0, 3.0)
    base = jnp.clip(jax.random.normal(noise_key, (SEQS, SEQ, QD)), -4.0, 4.0)
    result = base + 0.15 * common
    return result.astype(jnp.bfloat16)


def levels(stream_key, shape, cuts, smallest, largest):
    level = 1.0
    for dim, parts in cuts:
        steps = jax.random.uniform(jax.random.fold_in(jax.random.fold_in(stream_key, 6), dim), (parts,), jnp.float32, smallest / len(cuts), largest / len(cuts))
        level = level * jnp.repeat(jnp.exp(steps), shape[dim] // parts).reshape((-1,) + (1,) * (len(shape) - 1 - dim))
    return level


def normal_values(rng, dims, scale, most, cuts=(), kind=jnp.bfloat16):
    entries = scale * jax.random.normal(rng, dims, jnp.float32)
    if cuts:
        entries = entries * levels(rng, dims, cuts, -0.22, 0.18)
    return jnp.clip(entries, -most, most).astype(kind)


def setup_inputs(seed: int = 0) -> dict:
    key_of = jax.random.split(jax.random.key(seed), 16)
    normed = draw_normed(jax.random.fold_in(key_of[15], 71), 0)
    queries = draw_queries(jax.random.fold_in(key_of[15], 71), 0)
    keys = draw_keys(jax.random.fold_in(key_of[15], 71), 0)
    values = normal_values(key_of[3], (SEQS, SEQ, KVD), 1.0, 5.0, ((0, 8), (2, 32)))
    context_grad = draw_context_grad(jax.random.fold_in(key_of[15], 71), 0)
    segments = draw_segments(jax.random.fold_in(key_of[15], 71), 0)
    w_query = normal_values(key_of[6], (D, QD), D ** -0.5, 0.046875, ((0, 32),))
    w_key = normal_values(key_of[7], (D, KVD), D ** -0.5, 0.046875, ((0, 32),))
    w_value = normal_values(key_of[8], (D, KVD), D ** -0.5, 0.046875, ((0, 32),))
    adapter_down = normal_values(key_of[9], (3, RANK, D), D ** -0.5, 0.046875, ((2, 32),))
    up_query = normal_values(key_of[10], (RANK, QD), 0.1, 0.59765625, ((1, 32),))
    up_keyvalue = normal_values(key_of[11], (2, RANK, KVD), 0.03, 0.1796875, ((2, 32),))
    accum_down = normal_values(key_of[12], (3, RANK, D), 0.2, 1.2, ((1, 8), (2, 32)), jnp.float32)
    accum_query = normal_values(key_of[13], (RANK, QD), 0.05, 0.3, ((0, 8), (1, 32)), jnp.float32)
    accum_keyvalue = normal_values(key_of[14], (2, RANK, KVD), 0.1, 0.6, ((1, 8), (2, 32)), jnp.float32)
    return dict(normed=normed, queries=queries, keys=keys, values=values, context_grad=context_grad, segments=segments, w_query=w_query, w_key=w_key, w_value=w_value, adapter_down=adapter_down, up_query=up_query, up_keyvalue=up_keyvalue, accum_down=accum_down, accum_query=accum_query, accum_keyvalue=accum_keyvalue)


ADAPTER_SCALE = 2.0
ROPE_BASE = 500000.0
HIGH = lax.Precision.HIGHEST

def rotary_tables(length, width):
    exponent = jnp.arange(width // 2, dtype=jnp.float32) * (2.0 / width)
    frequency = 1.0 / ROPE_BASE ** exponent
    wavelength = 2.0 * math.pi / frequency
    blend = (8192.0 / wavelength - 1.0) / 3.0
    middle = (1.0 - blend) * frequency / 8.0 + blend * frequency
    scaled = jnp.where(wavelength < 2048.0, frequency, jnp.where(wavelength > 8192.0, frequency / 8.0, middle))
    angle = jnp.arange(length, dtype=jnp.float32)[:, None] * scaled[None, :]
    angle = jnp.concatenate([angle, angle], axis=1)
    return (jnp.cos(angle), jnp.sin(angle))

def unrotate(grads, cosine, sine):
    half_width = grads.shape[-1] // 2
    turned = grads * sine[:, None, :]
    flipped = jnp.concatenate([-turned[..., half_width:], turned[..., :half_width]], axis=-1)
    return grads * cosine[:, None, :] - flipped

def contract_last(left, right):
    return lax.dot_general(left, right, (((1,), (1,)), ((), ())), preferred_element_type=jnp.float32)

def reference(normed, queries, keys, values, context_grad, segments, w_query, w_key, w_value, adapter_down, up_query, up_keyvalue, accum_down, accum_query, accum_keyvalue):
    group_size = QH // KVH
    score_scale = 1.0 / math.sqrt(HD)
    cosine, sine = rotary_tables(SEQ, HD)
    positions = jnp.arange(SEQ, dtype=jnp.int32)

    def attend(item):
        query_seq, key_seq, value_seq, cot_seq, doc_ids = item
        query_heads = query_seq.astype(jnp.float32).reshape(SEQ, QH, HD)
        key_heads = jnp.tile(key_seq.astype(jnp.float32).reshape(SEQ, KVH, HD), (1, group_size, 1))
        value_heads = jnp.tile(value_seq.astype(jnp.float32).reshape(SEQ, KVH, HD), (1, group_size, 1))
        cotangent = cot_seq.astype(jnp.float32).reshape(SEQ, QH, HD)
        allowed = (positions[None, :] <= positions[:, None]) & (doc_ids[None, :] == doc_ids[:, None])
        scores = jnp.einsum('thd,shd->hts', query_heads, key_heads, precision=HIGH) * score_scale
        scores = jnp.where(allowed[None], scores, -jnp.inf)
        weights = jnp.exp(scores - lax.optimization_barrier(jnp.max(scores, axis=2, keepdims=True)))
        weights = weights / lax.optimization_barrier(jnp.sum(weights, axis=2, keepdims=True))
        attn_out = jnp.einsum('hts,shd->thd', weights, value_heads, precision=HIGH)
        row_delta = lax.optimization_barrier(jnp.sum(cotangent * attn_out, axis=2))
        weight_grad = jnp.einsum('thd,shd->hts', cotangent, value_heads, precision=HIGH)
        score_half = lax.optimization_barrier((weights * (weight_grad - row_delta.T[:, :, None])).astype(jnp.bfloat16)).astype(jnp.float32)
        weight_half = lax.optimization_barrier(weights.astype(jnp.bfloat16)).astype(jnp.float32)
        query_grad_rot = jnp.einsum('hts,shd->thd', score_half, key_heads, precision=HIGH) * score_scale
        key_grad_rot = jnp.einsum('hts,thd->shd', score_half, query_heads, precision=HIGH) * score_scale
        key_grad_rot = key_grad_rot.reshape(SEQ, group_size, KVH, HD).sum(axis=1)
        value_sum = jnp.einsum('hts,thd->shd', weight_half, cotangent, precision=HIGH)
        value_sum = value_sum.reshape(SEQ, group_size, KVH, HD).sum(axis=1)
        query_grad = unrotate(query_grad_rot, cosine, sine).astype(jnp.bfloat16).reshape(SEQ, QD)
        key_grad = unrotate(key_grad_rot, cosine, sine).astype(jnp.bfloat16).reshape(SEQ, KVD)
        value_grad = value_sum.astype(jnp.bfloat16).reshape(SEQ, KVD)
        return (query_grad, key_grad, value_grad)
    query_grad, key_grad, value_grad = lax.map(attend, (queries, keys, values, context_grad, segments))
    token_total = SEQS * SEQ
    query_flat = query_grad.reshape(token_total, QD)
    key_flat = key_grad.reshape(token_total, KVD)
    value_flat = value_grad.reshape(token_total, KVD)
    frozen_grad = contract_last(query_flat, w_query)
    frozen_grad = frozen_grad + contract_last(key_flat, w_key)
    frozen_grad = frozen_grad + contract_last(value_flat, w_value)
    normed_flat = normed.reshape(token_total, D)
    adapter_flat = adapter_down.reshape(3 * RANK, D)
    down_half = contract_last(normed_flat, adapter_flat).astype(jnp.bfloat16)
    up_grad = ADAPTER_SCALE * jnp.concatenate([contract_last(query_flat, up_query), contract_last(key_flat, up_keyvalue[0]), contract_last(value_flat, up_keyvalue[1])], axis=1)
    up_half = up_grad.astype(jnp.bfloat16)
    input_grad = frozen_grad + jnp.dot(up_half, adapter_flat, preferred_element_type=jnp.float32)
    input_grad = input_grad.astype(jnp.bfloat16).reshape(SEQS, SEQ, D)
    grad_down = jnp.dot(up_grad.T, normed_flat.astype(jnp.float32), precision=HIGH).reshape(3, RANK, D)
    grad_query = ADAPTER_SCALE * jnp.dot(down_half[:, :RANK].T, query_flat, preferred_element_type=jnp.float32)
    grad_keyvalue = ADAPTER_SCALE * jnp.stack([jnp.dot(down_half[:, RANK:2 * RANK].T, key_flat, preferred_element_type=jnp.float32), jnp.dot(down_half[:, 2 * RANK:].T, value_flat, preferred_element_type=jnp.float32)])
    return (input_grad, accum_down + grad_down / token_total, accum_query + grad_query / token_total, accum_keyvalue + grad_keyvalue / token_total)
```

```python
import functools
import math

import jax
import jax.numpy as jnp
import numpy as np
from jax import lax
from jax.experimental import pallas as pl
from jax.experimental.pallas import tpu as pltpu
from jax.sharding import PartitionSpec as P

HD = 128
RANK = 16
ADAPTER_SCALE = 2.0
ROPE_BASE = 500000.0
F32 = jnp.float32
BF16 = jnp.bfloat16
MESH = pl.DeviceIdType.MESH

NY, NZ = 4, 4
NT = NY * NZ * 2
HALF = NT // 2
T = 256
QC = 256
NC = 512


def rotary_tables():
    exponent = np.arange(HD // 2, dtype=np.float32) * np.float32(2.0 / HD)
    frequency = (1.0 / np.float32(ROPE_BASE) ** exponent).astype(np.float32)
    wavelength = (2.0 * math.pi / frequency).astype(np.float32)
    blend = (8192.0 / wavelength - 1.0) / 3.0
    middle = (1.0 - blend) * frequency / 8.0 + blend * frequency
    scaled = np.where(
        wavelength < 2048.0, frequency, np.where(wavelength > 8192.0, frequency / 8.0, middle)
    ).astype(np.float32)
    angle = np.arange(T, dtype=np.float32)[:, None] * scaled[None, :]
    cosine = np.cos(angle).astype(np.float32)
    sine = np.sin(angle).astype(np.float32)
    rows = np.stack(
        [np.concatenate([cosine, cosine], 1), np.concatenate([sine, -sine], 1)]
    )
    cols = np.stack([cosine.T, sine.T])
    return rows, cols


def nt(left, right):
    return lax.dot_general(left, right, (((1,), (1,)), ((), ())), preferred_element_type=F32)


def nn(left, right):
    return lax.dot_general(left, right, (((1,), (0,)), ((), ())), preferred_element_type=F32)


def tn(left, right):
    return lax.dot_general(left, right, (((0,), (0,)), ((), ())), preferred_element_type=F32)


def picks(rows, cols, first, offset):
    a = lax.broadcasted_iota(jnp.int32, (rows, cols), 0)
    col = lax.broadcasted_iota(jnp.int32, (rows, cols), 1)
    e = (a & 7) - first
    hit = (e >= 0) & (e < 2) & (col == offset + 2 * (a >> 3) + e)
    return jnp.where(hit, 1.0, 0.0).astype(BF16)


def kernel(
    ndp,
    normed_h, queries_h, keys_h, values_h, cot_h, seg_h, wq_h, wk_h, wv_h,
    adown_h, upq_h, upkv_h, accd_h, accq_h, acckv_h, tab_h, tabt_h,
    out_i, out_d, out_q, out_kv,
    normed, queries, cot, seg, wq, wkv, adown, upq, upkv, accd, accq, acckv, tab, tabt,
    kvown, kvt, rs_src, rs_dst, qall, kvg, ps_src, ps_in, ps_all, pay, dp_in, acc, bias,
    lsem, wsem, kvs, kvr, rss, rsr, qs, qr, gs, gr, pss, psr, pas, par, dps, dpr,
):
    i = lax.axis_index("tensor")
    b = lax.axis_index("dp")
    core = i % 2
    z = (i // 2) % NZ
    y = i // (2 * NZ)
    side = i // HALF
    own_in = core == side

    def dev(dy, dz, dc):
        return (((y + dy) % NY) * NZ + (z + dz) % NZ) * 2 + (core + dc) % 2

    loads = [
        (keys_h, kvown.at[0]), (values_h, kvown.at[1]), (queries_h.at[0], queries),
        (cot_h.at[0], cot), (seg_h, seg), (normed_h.at[0], normed), (adown_h, adown),
        (upq_h, upq), (upkv_h, upkv), (tab_h, tab), (tabt_h, tabt),
        (accd_h, accd), (accq_h, accq), (acckv_h, acckv), (wk_h, wkv.at[0]), (wv_h, wkv.at[1]),
    ]
    loads = [pltpu.make_async_copy(src, dst, lsem.at[n]) for n, (src, dst) in enumerate(loads)]
    for copy in loads:
        copy.start()

    barrier = pltpu.get_barrier_semaphore()

    def greet_t(k, _):
        pl.semaphore_signal(
            barrier, 1, device_id=(b, (i + 1 + k) % NT), device_id_type=MESH
        )
        return 0

    def greet_d(k, _):
        pl.semaphore_signal(
            barrier, 1, device_id=((b + 1 + k) % ndp, i), device_id_type=MESH
        )
        return 0

    lax.fori_loop(0, NT - 1, greet_t, 0)
    lax.fori_loop(0, ndp - 1, greet_d, 0)

    def load_w(k, _):
        pltpu.make_async_copy(
            wq_h.at[:, pl.ds(pl.multiple_of(k * QC, QC), QC)], wq.at[k], wsem
        ).start()
        return 0

    lax.fori_loop(0, NT, load_w, 0)

    def remote(src, dst, send, recv, to):
        return pltpu.make_async_remote_copy(
            src_ref=src, dst_ref=dst, send_sem=send, recv_sem=recv,
            device_id=to, device_id_type=MESH,
        )

    def drain(ref, sem):
        pltpu.make_async_copy(ref, ref, sem).wait()

    loads[0].wait()
    loads[1].wait()
    pl.semaphore_wait(barrier, NT - 1 + ndp - 1)

    home = pl.ds(pl.multiple_of((i % HALF) * 16, 16), 16)

    def send_kv(m, _):
        to = 2 * m + side

        @pl.when(to != i)
        def _():
            remote(kvown, kvt.at[:, home, :], kvs, kvr, (b, to)).start()

        return 0

    lax.fori_loop(0, HALF, send_kv, 0)

    @pl.when(own_in)
    def _():
        kvt[:, home, :] = kvown[...]

    loads[4].wait()
    doc = jnp.broadcast_to(seg[...].astype(F32), (T, T))
    row = lax.broadcasted_iota(jnp.int32, (T, T), 0)
    col = lax.broadcasted_iota(jnp.int32, (T, T), 1)
    bias[...] = jnp.where((col <= row) & (doc == doc.T), 0.0, -jnp.inf)
    loads[5].wait()
    loads[6].wait()
    down_part = nt(adown[...].reshape(3 * RANK, NC), normed[...])
    for n in range(2):
        ps_src[n, 64:112, :] = down_part[:, n * 128 : (n + 1) * 128]
        ps_src[n, 112:128, :] = jnp.zeros((16, 128), F32)
    for n in (2, 3, 7, 8, 9, 10):
        loads[n].wait()

    def wait_16(sem, part, whole):
        @pl.when(own_in)
        def _():
            drain(part, sem)

        @pl.when(jnp.logical_not(own_in))
        def _():
            drain(whole, sem)

    wait_16(kvr, kvt.at[:, 0:240, :], kvt)

    scale = 1.0 / math.sqrt(HD)
    for h in range(2):
        cols = slice(h * HD, (h + 1) * HD)
        q, g = queries[:, cols], cot[:, cols]
        kt, vt = kvt[0, cols, :], kvt[1, cols, :]
        scores = nn(q, kt) * scale + bias[...]
        weights = jnp.exp(scores - jnp.max(scores, axis=1, keepdims=True))
        weights = weights / jnp.sum(weights, axis=1, keepdims=True)
        weight_grad = nn(g, vt)
        delta = jnp.sum(weights * weight_grad, axis=1, keepdims=True)
        score_grad = (weights * (weight_grad - delta)).astype(BF16)
        query_rot = nt(score_grad, kt) * scale
        qall[i, :, cols] = (
            query_rot * tab[0] + pltpu.roll(query_rot, HD // 2, 1) * tab[1]
        ).astype(BF16)
        key_rot = tn(q, score_grad) * scale
        one, two = key_rot[: HD // 2], key_rot[HD // 2 :]
        cosine, sine = tabt[0], tabt[1]
        rs_src[0, cols, :] = jnp.concatenate(
            [one * cosine + two * sine, two * cosine - one * sine], axis=0
        ).astype(BF16)
        rs_src[1, cols, :] = tn(g, weights.astype(BF16)).astype(BF16)

    def send_rs(m, _):
        to = HALF * core + m

        @pl.when(to != i)
        def _():
            remote(
                rs_src.at[:, pl.ds(pl.multiple_of(16 * m, 16), 16), :],
                rs_dst.at[i // 2], rss, rsr, (b, to),
            ).start()

        return 0

    lax.fori_loop(0, HALF, send_rs, 0)

    @pl.when(own_in)
    def _():
        rs_dst[i // 2] = rs_src[:, home, :]

    def q_ref(slot, part):
        if part is None:
            return qall.at[slot]
        return qall.at[slot, pl.ds(part * (T // 2), T // 2), :]

    def g_ref(slot, part):
        rows = pl.ds(pl.multiple_of(slot * 16, 16), 16)
        if part is None:
            return kvg.at[:, rows, :]
        return kvg.at[part, rows, :]

    class Gather:
        def __init__(self, ref, send, recv):
            self.ref, self.s, self.r = ref, send, recv

        def push(self, slot, to, part=None):
            ref = self.ref(slot, part)
            remote(ref, ref, self.s, self.r.at[slot], (b, to)).start()

        def wait(self, slot):
            drain(self.ref(slot, None), self.r.at[slot])

        def first(self):
            own = dev(0, 0, 0)
            for to in (dev(0, 1, 0), dev(0, -1, 0), dev(1, 0, 0), dev(-1, 0, 0), dev(0, 0, 1)):
                self.push(own, to)

        def column(self, dz):
            slot = dev(0, dz, 0)
            self.wait(slot)
            if dz in (1, -1):
                self.push(slot, dev(0, -dz, 0), 0 if dz == -1 else 1)
            for to in (dev(1, 0, 0), dev(-1, 0, 0), dev(0, 0, 1)):
                self.push(slot, to)

        def spread(self, dz):
            for dy in (-1, 1):
                slot = dev(dy, dz, 0)
                self.wait(slot)
                self.push(slot, dev(-dy, 0, 0), 0 if dy == -1 else 1)
                self.push(slot, dev(0, 0, 1))

        def last(self, dz):
            slot = dev(2, dz, 0)
            self.wait(slot)
            self.push(slot, dev(0, 0, 1))

    query = Gather(q_ref, qs, qr)
    keyvalue = Gather(g_ref, gs, gr)
    query.first()

    up_rows = nn(picks(64, RANK, 0, 0), upq[...]).astype(BF16)
    up_part = nt(up_rows, qall[i])

    wait_16(rsr, rs_dst.at[0:15], rs_dst)
    total = rs_dst[0].astype(F32)
    for n in range(1, HALF):
        total = total + rs_dst[n].astype(F32)
    total = total.astype(BF16)
    mine = pl.ds(pl.multiple_of(i * 16, 16), 16)
    kvg[:, mine, :] = total
    keyvalue.first()
    for p in range(2):
        up_rows = nn(picks(64, RANK, 2 + 2 * p, 0), upkv[p]).astype(BF16)
        up_part = up_part + nn(up_rows, total[p])
    up_part = ADAPTER_SCALE * up_part
    for n in range(2):
        ps_src[n, 0:64, :] = up_part[:, n * 128 : (n + 1) * 128]

    def part_of(j):
        return j % 2, pl.ds(pl.multiple_of(8 * (j // 2), 8), 8)

    def send_ps(k, _):
        to = (i + 1 + k) % NT
        half, rows = part_of(to)
        remote(ps_src.at[half, rows, :], ps_in.at[i], pss, psr, (b, to)).start()
        return 0

    lax.fori_loop(0, NT - 1, send_ps, 0)
    my_half, my_rows = part_of(i)
    ps_in[i] = ps_src[my_half, my_rows, :]

    query.spread(0)
    query.column(-1)
    query.column(1)

    drain(wq, wsem)
    acc[...] = jnp.zeros_like(acc)

    def times(slot):
        acc[...] += nt(qall[slot], wq[slot])

    def project(dz):
        query.last(dz)

        def near(k, _):
            times(dev(k, dz, 0))
            return 0

        lax.fori_loop(0, NY, near, 0)

        def far(k, _):
            slot = dev(k, dz, 1)
            query.wait(slot)
            times(slot)
            return 0

        lax.fori_loop(0, NY, far, 0)

    drain(ps_in.at[0 : NT - 1], psr)
    ps_all[my_half, my_rows, :] = jnp.sum(ps_in[...], axis=0)

    def send_pa(k, _):
        to = (i + 1 + k) % NT
        ref = ps_all.at[my_half, my_rows, :]
        remote(ref, ref, pas, par, (b, to)).start()
        return 0

    lax.fori_loop(0, NT - 1, send_pa, 0)

    keyvalue.spread(0)
    keyvalue.column(-1)
    keyvalue.column(1)
    query.spread(-1)
    query.spread(1)
    query.column(2)
    project(0)
    keyvalue.last(0)
    keyvalue.spread(-1)
    keyvalue.spread(1)
    keyvalue.column(2)

    drain(ps_in.at[0 : NT - 1], par)
    sums = jnp.concatenate([ps_all[0], ps_all[1]], axis=1)
    up_sum = sums[0:64]
    down_half = sums[64:112].astype(BF16)
    high = up_sum.astype(BF16)
    rest = up_sum - high.astype(F32)
    middle = rest.astype(BF16)
    low = (rest - middle.astype(F32)).astype(BF16)
    down_grad = nn(high, normed[...]) + (nn(middle, normed[...]) + nn(low, normed[...]))
    downs = [
        nn(picks(64, 3 * RANK, 6, p * RANK), down_half).astype(BF16) for p in range(3)
    ]
    pay[...] = down_grad
    pay[:, 0:QC] += nn(downs[0], qall[i])
    for p in range(2):
        start = QC + p * 128
        pay[:, start : start + 16] += nt(downs[1 + p], kvg[p, mine, :])

    def send_dp(k, _):
        to = (b + 1 + k) % ndp
        remote(
            pay.at[pl.ds(pl.multiple_of(8 * to, 8), 8), :], dp_in.at[b], dps, dpr, (to, i)
        ).start()
        return 0

    lax.fori_loop(0, ndp - 1, send_dp, 0)
    dp_in[b] = pay[pl.ds(pl.multiple_of(8 * b, 8), 8), :]

    query.last(-1)
    query.last(1)
    query.spread(2)

    def project_rest(dz):
        def near(k, _):
            times(dev(k, dz, 0))
            return 0

        lax.fori_loop(0, NY, near, 0)

        def far(k, _):
            slot = dev(k, dz, 1)
            query.wait(slot)
            times(slot)
            return 0

        lax.fori_loop(0, NY, far, 0)

    project_rest(-1)
    project_rest(1)
    keyvalue.last(-1)
    keyvalue.last(1)
    keyvalue.spread(2)
    query.last(2)
    keyvalue.last(2)

    def far_kv(k, _):
        keyvalue.wait(2 * k + 1 - core)
        return 0

    lax.fori_loop(0, HALF, far_kv, 0)
    for n in (14, 15):
        loads[n].wait()
    adown_rows = nn(
        picks(64, 3 * RANK, 0, 0) + picks(64, 3 * RANK, 2, RANK) + picks(64, 3 * RANK, 4, 2 * RANK),
        adown[...].reshape(3 * RANK, NC),
    ).astype(BF16)
    for p in range(2):
        acc[...] += lax.dot_general(
            kvg[p], wkv[p], (((0,), (1,)), ((), ())), preferred_element_type=F32
        )
    acc[...] += tn(high, adown_rows)
    project_rest(2)
    out_i[0] = acc[...].astype(BF16)

    for n in (11, 12, 13):
        loads[n].wait()
    if ndp > 1:
        drain(dp_in.at[0 : ndp - 1], dpr)
    total = dp_in[0]
    for n in range(1, ndp):
        total = total + dp_in[n]
    tokens = float(ndp * T)
    for p in range(3):
        out_d[p] = accd[p] + total[2 * p : 2 * p + 2, :] / tokens
    out_q[...] = accq[...] + ADAPTER_SCALE * total[6:8, 0:QC] / tokens
    for p in range(2):
        start = QC + p * 128
        out_kv[p] = acckv[p] + ADAPTER_SCALE * total[6:8, start : start + 16] / tokens

    wait_16(kvs, kvt.at[:, 0:240, :], kvt)
    wait_16(rss, rs_dst.at[0:15], rs_dst)
    drain(qall.at[0 : NT - 1], qs)
    drain(kvg.at[:, 0 : 16 * (NT - 1), :], gs)
    drain(ps_in.at[0 : NT - 1], pss)
    drain(ps_in.at[0 : NT - 1], pas)
    if ndp > 1:
        drain(dp_in.at[0 : ndp - 1], dps)


def per_device(
    ndp, normed, queries, keys, values, context_grad, segments, w_query, w_key, w_value,
    adapter_down, up_query, up_keyvalue, accum_down, accum_query, accum_keyvalue,
):
    tab, tabt = rotary_tables()
    keys_t = jnp.transpose(keys[0])
    values_t = jnp.transpose(values[0])
    vmem = pltpu.VMEM
    dma = pltpu.SemaphoreType.DMA
    scratch = [
        vmem((T, NC), BF16),
        vmem((T, QC), BF16),
        vmem((T, QC), BF16),
        vmem((1, T), jnp.int32),
        vmem((NT, NC, QC), BF16),
        vmem((2, NC, 512), BF16),
        vmem((3, RANK, NC), BF16),
        vmem((RANK, QC), BF16),
        vmem((2, RANK, 16), BF16),
        vmem(accum_down.shape, F32),
        vmem(accum_query.shape, F32),
        vmem(accum_keyvalue.shape, F32),
        vmem(tab.shape, F32),
        vmem(tabt.shape, F32),
        vmem((2, 16, T), BF16),
        vmem((2, 2 * HD, T), BF16),
        vmem((2, 2 * HD, T), BF16),
        vmem((HALF, 2, 16, T), BF16),
        vmem((NT, T, QC), BF16),
        vmem((2, 512, T), BF16),
        vmem((2, 128, 128), F32),
        vmem((NT, 8, 128), F32),
        vmem((2, 128, 128), F32),
        vmem((64, NC), F32),
        vmem((8, 8, NC), F32),
        vmem((T, NC), F32),
        vmem((T, T), F32),
        dma((16,)), dma,
        dma, dma, dma, dma,
        dma, dma((NT,)), dma, dma((NT,)),
        dma, dma, dma, dma, dma, dma,
    ]
    out_shape = (
        jax.ShapeDtypeStruct((1, T, NC), BF16),
        jax.ShapeDtypeStruct(accum_down.shape, F32),
        jax.ShapeDtypeStruct(accum_query.shape, F32),
        jax.ShapeDtypeStruct(accum_keyvalue.shape, F32),
    )
    return pl.pallas_call(
        functools.partial(kernel, ndp),
        out_shape=out_shape,
        in_specs=[pl.BlockSpec(memory_space=pl.ANY)] * 17,
        out_specs=tuple(pl.BlockSpec(memory_space=pltpu.VMEM) for _ in out_shape),
        scratch_shapes=scratch,
        compiler_params=pltpu.CompilerParams(
            collective_id=0, has_side_effects=True, vmem_limit_bytes=64 * 1024 * 1024 - 288 * 1024
        ),
    )(
        normed, queries, keys_t, values_t, context_grad, segments, w_query, w_key, w_value,
        adapter_down, up_query, up_keyvalue, accum_down, accum_query, accum_keyvalue,
        jnp.asarray(tab), jnp.asarray(tabt),
    )


def solution(mesh):
    in_specs = (
        P("dp", None, "tensor"),
        P("dp", None, "tensor"),
        P("dp", None, "tensor"),
        P("dp", None, "tensor"),
        P("dp", None, "tensor"),
        P("dp", None),
        P("tensor", None),
        P("tensor", None),
        P("tensor", None),
        P(None, None, "tensor"),
        P(None, "tensor"),
        P(None, None, "tensor"),
        P(None, "dp", "tensor"),
        P("dp", "tensor"),
        P(None, "dp", "tensor"),
    )
    out_specs = (
        P("dp", None, "tensor"),
        P(None, "dp", "tensor"),
        P("dp", "tensor"),
        P(None, "dp", "tensor"),
    )
    return jax.shard_map(
        functools.partial(per_device, mesh.shape["dp"]),
        mesh=mesh, in_specs=in_specs, out_specs=out_specs, check_vma=False,
    )
```

```python
import functools
import math

import jax
import jax.numpy as jnp
import numpy as np
from jax import lax
from jax.experimental import pallas as pl
from jax.experimental.pallas import tpu as pltpu
from jax.sharding import PartitionSpec as P

HD = 128
RANK = 16
ADAPTER_SCALE = 2.0
ROPE_BASE = 500000.0
F32 = jnp.float32
BF16 = jnp.bfloat16
MESH = pl.DeviceIdType.MESH

NY, NZ = 4, 4
NT = NY * NZ * 2
HALF = NT // 2
T = 256
QC = 256
NC = 512


def rotary_tables():
    exponent = np.arange(HD // 2, dtype=np.float32) * np.float32(2.0 / HD)
    frequency = (1.0 / np.float32(ROPE_BASE) ** exponent).astype(np.float32)
    wavelength = (2.0 * math.pi / frequency).astype(np.float32)
    blend = (8192.0 / wavelength - 1.0) / 3.0
    middle = (1.0 - blend) * frequency / 8.0 + blend * frequency
    scaled = np.where(
        wavelength < 2048.0, frequency, np.where(wavelength > 8192.0, frequency / 8.0, middle)
    ).astype(np.float32)
    angle = np.arange(T, dtype=np.float32)[:, None] * scaled[None, :]
    cosine = np.cos(angle).astype(np.float32)
    sine = np.sin(angle).astype(np.float32)
    rows = np.stack(
        [np.concatenate([cosine, cosine], 1), np.concatenate([sine, -sine], 1)]
    )
    cols = np.stack([cosine.T, sine.T])
    return rows, cols


def nt(left, right):
    return lax.dot_general(left, right, (((1,), (1,)), ((), ())), preferred_element_type=F32)


def nn(left, right):
    return lax.dot_general(left, right, (((1,), (0,)), ((), ())), preferred_element_type=F32)


def tn(left, right):
    return lax.dot_general(left, right, (((0,), (0,)), ((), ())), preferred_element_type=F32)


CHUNKS = ((0, 256, "z"),)

ORDER = (
    ("first", 0), ("up",), ("fwd", 0, 0), ("w",), ("mm", 0, 0), ("rsy",), ("spr", 0, 0, 1),
    ("spr", 0, 0, -1), ("fwd", 1, 0), ("fwd", -1, 0), ("mm", 1, 0), ("mm", -1, 0),
    ("col", 0, 1), ("col", 0, -1), ("fwd", 0, 1), ("fwd", 0, -1), ("fwd", 2, 0), ("mm", 0, 1),
    ("mm", 0, -1), ("mm", 2, 0), ("up2",), ("rsz",), ("first", "g"), ("gfwd", 0, 0),
    ("spr", 0, 1, 1), ("spr", 0, 1, -1), ("fwd", 1, 1), ("fwd", -1, 1), ("col", 0, 2),
    ("fwd", 0, 2), ("mm", 1, 1), ("mm", -1, 1), ("mm", 0, 2), ("spr", 0, -1, 1),
    ("spr", 0, -1, -1), ("col", "g", 1), ("col", "g", -1), ("gfwd", 0, 1), ("gfwd", 0, -1),
    ("spr", "g", 0, 1), ("spr", "g", 0, -1), ("gfwd", 1, 0), ("gfwd", -1, 0), ("fwd", 1, -1),
    ("fwd", -1, -1), ("fwd", 2, 1), ("mm", 1, -1), ("mm", -1, -1), ("dp",), ("col", "g", 2),
    ("gfwd", 0, 2), ("mm", 2, 1), ("spr", 0, 2, 1), ("spr", 0, 2, -1), ("fwd", 1, 2),
    ("fwd", -1, 2), ("fwd", 2, -1), ("spr", "g", 1, 1), ("spr", "g", 1, -1), ("gfwd", 1, 1),
    ("gfwd", -1, 1), ("spr", "g", -1, 1), ("spr", "g", -1, -1), ("gfwd", 2, 0), ("gfwd", 1, -1),
    ("spr", "g", 2, 1), ("spr", "g", 2, -1), ("gfwd", -1, -1), ("gfwd", 1, 2), ("gfwd", -1, 2),
    ("mm", 2, -1), ("mm", 1, 2), ("fwd", 2, 2), ("mm", -1, 2), ("gfwd", 2, 1), ("gfwd", 2, -1),
    ("gfwd", 2, 2), ("mm", 2, 2), ("dpout",), ("kv",),
)


def kernel(
    ndp,
    normed_h, queries_h, keys_h, values_h, cot_h, seg_h, wq_h, wk_h, wv_h,
    adown_h, upq_h, upkv_h, accd_h, accq_h, acckv_h, tab_h, tabt_h,
    out_i, out_d, out_q, out_kv,
    normed, queries, cot, seg, wq, wkv, adown, upq, upkv, accd, accq, acckv, tab, tabt,
    kvown, kt, vt, utown, ut, rs_src, rsy, rsz, rs_dst, qall, kvg, ps_src, ps_in, ps_all,
    pay, dp_in, acc, bias, ob, od, oq, okv,
    lsem, wsem, kvs, kvr, uts, utr, rys, ryr, rzs, rzr, qs, qr, fs, fr, gs, gr,
    pss, psr, pas, par, dps, dpr, osem,
):
    i = lax.axis_index("tensor")
    b = lax.axis_index("dp")
    core = i % 2
    z = (i // 2) % NZ
    y = i // (2 * NZ)
    side = i // HALF
    own_in = core == side

    def dev(dy, dz, dc):
        return (((y + dy) % NY) * NZ + (z + dz) % NZ) * 2 + (core + dc) % 2

    loads = [
        (keys_h, kvown.at[0]), (values_h, kvown.at[1]), (queries_h.at[0], queries),
        (cot_h.at[0], cot), (seg_h, seg), (normed_h.at[0], normed), (adown_h, adown),
        (upq_h, upq), (upkv_h, upkv), (tab_h, tab), (tabt_h, tabt),
        (accd_h, accd), (accq_h, accq), (acckv_h, acckv), (wk_h, wkv.at[0]), (wv_h, wkv.at[1]),
    ]
    loads = [pltpu.make_async_copy(src, dst, lsem.at[n]) for n, (src, dst) in enumerate(loads)]
    for copy in loads:
        copy.start()

    barrier = pltpu.get_barrier_semaphore()

    def greet_t(k, _):
        pl.semaphore_signal(
            barrier, 1, device_id=(b, (i + 1 + k) % NT), device_id_type=MESH
        )
        return 0

    def greet_d(k, _):
        pl.semaphore_signal(
            barrier, 1, device_id=((b + 1 + k) % ndp, i), device_id_type=MESH
        )
        return 0

    lax.fori_loop(0, NT - 1, greet_t, 0)
    lax.fori_loop(0, ndp - 1, greet_d, 0)

    def load_w(k, _):
        pltpu.make_async_copy(
            wq_h.at[:, pl.ds(pl.multiple_of(k * QC, QC), QC)], wq.at[k], wsem
        ).start()
        return 0

    lax.fori_loop(0, NT, load_w, 0)

    def remote(src, dst, send, recv, to):
        return pltpu.make_async_remote_copy(
            src_ref=src, dst_ref=dst, send_sem=send, recv_sem=recv,
            device_id=to, device_id_type=MESH,
        )

    def drain(ref, sem):
        pltpu.make_async_copy(ref, ref, sem).wait()

    def by(test, sem, part, whole):
        @pl.when(test)
        def _():
            drain(part, sem)

        @pl.when(jnp.logical_not(test))
        def _():
            drain(whole, sem)

    owner = (i < 24) & (core == (i // 2) % 2)

    class Sums:
        def __init__(self, k):
            self.src, self.into, self.all = ps_src.at[k], ps_in.at[k], ps_all.at[k]
            self.sems = pss.at[k], psr.at[k], pas.at[k], par.at[k]

        def piece(self, ref, n):
            return ref.at[n % 2, pl.ds(pl.multiple_of(8 * (n // 2), 8), 8), :]

        def scatter(self, value):
            for n in range(2):
                self.src[n] = value[:, n * 128 : (n + 1) * 128]

            def send(n, _):
                to = 2 * n + n % 2

                @pl.when(to != i)
                def _():
                    remote(
                        self.piece(self.src, n), self.into.at[i],
                        self.sems[0], self.sems[1], (b, to),
                    ).start()

                return 0

            lax.fori_loop(0, 12, send, 0)

        def reduce(self):
            @pl.when(owner)
            def _():
                n = i // 2
                rows = pl.ds(pl.multiple_of(8 * (n // 2), 8), 8)
                self.into[i] = self.src[n % 2, rows, :]
                drain(self.into.at[0 : NT - 1], self.sems[1])
                self.all[n % 2, rows, :] = jnp.sum(self.into[...], axis=0)

                def send(k, _):
                    ref = self.piece(self.all, n)
                    remote(
                        ref, ref, self.sems[2], self.sems[3], (b, (i + 1 + k) % NT)
                    ).start()
                    return 0

                lax.fori_loop(0, NT - 1, send, 0)

        def result(self):
            by(owner, self.sems[3], self.into.at[0:11], self.into.at[0:12])
            return jnp.concatenate([self.all[0], self.all[1]], axis=1)

        def finish(self):
            by(owner, self.sems[0], self.into.at[0:11], self.into.at[0:12])

            @pl.when(owner)
            def _():
                drain(self.into.at[0 : NT - 1], self.sems[2])

    downs, ups = Sums(0), Sums(1)

    loads[0].wait()
    loads[1].wait()
    pl.semaphore_wait(barrier, NT - 1 + ndp - 1)

    home = pl.ds(pl.multiple_of((i % HALF) * 16, 16), 16)

    def scatter_home(src, dst, send, recv):
        def one(m, _):
            to = 2 * m + side

            @pl.when(to != i)
            def _():
                remote(src, dst.at[home, :], send, recv, (b, to)).start()

            return 0

        lax.fori_loop(0, HALF, one, 0)

        @pl.when(own_in)
        def _():
            dst[home, :] = src[...]

    scatter_home(kvown.at[0], kt, kvs.at[0], kvr.at[0])
    scatter_home(kvown.at[1], vt, kvs.at[1], kvr.at[1])

    loads[5].wait()
    loads[6].wait()
    downs.scatter(nt(adown[...].reshape(3 * RANK, NC), normed[...]))
    loads[8].wait()
    rank = lax.broadcasted_iota(jnp.int32, (RANK, 128), 0)
    lane = lax.broadcasted_iota(jnp.int32, (RANK, 128), 1)
    columns = jnp.zeros((16, 128), F32)
    for p in range(2):
        place = jnp.where(lane == rank + p * RANK, 1.0, 0.0).astype(BF16)
        columns = columns + tn(upkv[p], place)
    utown[...] = columns.astype(BF16)
    scatter_home(utown, ut, uts, utr)
    loads[4].wait()
    doc = jnp.broadcast_to(seg[...].astype(F32), (T, T))
    row = lax.broadcasted_iota(jnp.int32, (T, T), 0)
    col = lax.broadcasted_iota(jnp.int32, (T, T), 1)
    bias[...] = jnp.where((col <= row) & (doc == doc.T), 0.0, -jnp.inf)
    acc[...] = jnp.zeros_like(acc)
    for n in (2, 3, 7, 9, 10):
        loads[n].wait()

    def send_rsy(p):
        for h in range(2):
            to = ((2 * core + h) * NZ + z) * 2 + core

            @pl.when(to != i)
            def _():
                remote(rs_src.at[p, h], rsy.at[p, y], rys.at[p], ryr.at[p], (b, to)).start()

            @pl.when(to == i)
            def _():
                rsy[p, y] = rs_src[p, h]

    scale = 1.0 / math.sqrt(HD)
    heads = [slice(0, HD), slice(HD, 2 * HD)]
    by(own_in, kvr.at[0], kt.at[0:240, :], kt)
    probs = []
    for h in heads:
        scores = nn(queries[:, h], kt[h, :]) * scale + bias[...]
        weights = jnp.exp(scores - jnp.max(scores, axis=1, keepdims=True))
        probs.append(weights / jnp.sum(weights, axis=1, keepdims=True))
    for n, h in enumerate(heads):
        rs_src[1, n] = tn(cot[:, h], probs[n].astype(BF16)).astype(BF16)
    send_rsy(1)
    by(own_in, kvr.at[1], vt.at[0:240, :], vt)
    score_grads = []
    cosine, sine = tabt[0], tabt[1]
    for n, h in enumerate(heads):
        weight_grad = nn(cot[:, h], vt[h, :])
        delta = jnp.sum(probs[n] * weight_grad, axis=1, keepdims=True)
        score_grads.append((probs[n] * (weight_grad - delta)).astype(BF16))
        key_rot = tn(queries[:, h], score_grads[n]) * scale
        one, two = key_rot[: HD // 2], key_rot[HD // 2 :]
        rs_src[0, n] = jnp.concatenate(
            [one * cosine + two * sine, two * cosine - one * sine], axis=0
        ).astype(BF16)
    send_rsy(0)
    for n, h in enumerate(heads):
        query_rot = nt(score_grads[n], kt[h, :]) * scale
        qall[i, :, h] = (
            query_rot * tab[0] + pltpu.roll(query_rot, HD // 2, 1) * tab[1]
        ).astype(BF16)

    class Gather:
        def __init__(self, axis, ref, send, recv):
            self.axis, self.ref, self.s, self.r = axis, ref, send, recv

        def at(self, d, e):
            return dev(e, d, 0) if self.axis == "z" else dev(d, e, 0)

        def push(self, slot, to, part=None):
            ref = self.ref(slot, part)
            remote(ref, ref, self.s, self.r.at[slot], (b, to)).start()

        def wait(self, slot):
            drain(self.ref(slot, None), self.r.at[slot])

        def first(self):
            for d, e in ((1, 0), (-1, 0), (0, 1), (0, -1)):
                self.push(i, self.at(d, e))

        def col(self, d):
            slot = self.at(d, 0)
            self.wait(slot)
            if d != 2:
                self.push(slot, self.at(-d, 0), 0 if d == -1 else 1)
            for e in (1, -1):
                self.push(slot, self.at(0, e))

        def spr(self, d, e):
            slot = self.at(d, e)
            self.wait(slot)
            self.push(slot, self.at(0, -e), 0 if e == -1 else 1)

        def far(self, dy, dz):
            if (dy if self.axis == "z" else dz) == 2:
                self.wait(dev(dy, dz, 0))

    def q_ref(first, last):
        half = (last - first) // 2

        def ref(slot, part):
            if part is None:
                return qall.at[slot, pl.ds(first, last - first), :]
            return qall.at[slot, pl.ds(first + part * half, half), :]

        return ref

    def g_ref(slot, part):
        rows = pl.ds(pl.multiple_of(slot * 16, 16), 16)
        if part is None:
            return kvg.at[:, rows, :]
        return kvg.at[part, rows, :]

    gathers = {
        n: Gather(axis, q_ref(first, last), qs.at[n], qr.at[n])
        for n, (first, last, axis) in enumerate(CHUNKS)
    }
    gathers["g"] = Gather("z", g_ref, gs.at[0], gr)
    mine = pl.ds(pl.multiple_of(i * 16, 16), 16)
    other = i + 1 - 2 * core

    def step_first(tag):
        gathers[tag].first()

    def step_col(tag, d):
        gathers[tag].col(d)

    def step_spr(tag, d, e):
        gathers[tag].spr(d, e)

    def step_fwd(dy, dz):
        slot = dev(dy, dz, 0)
        for n in range(len(CHUNKS)):
            gathers[n].far(dy, dz)
        remote(qall.at[slot], qall.at[slot], fs, fr.at[slot], (b, other)).start()

    def step_gfwd(dy, dz):
        gathers["g"].far(dy, dz)
        ref = g_ref(dev(dy, dz, 0), None)
        remote(ref, ref, gs.at[1], gr.at[dev(dy, dz, 0)], (b, other)).start()

    def step_mm(dy, dz):
        one, two = dev(dy, dz, 0), dev(dy, dz, 1)
        drain(qall.at[two], fr.at[two])
        acc[...] += nt(qall[one], wq[one]) + nt(qall[two], wq[two])

    def step_up():
        by(own_in, utr, ut.at[0:240, :], ut)
        sums = [nt(upq[...], qall[i])]
        for p in range(2):
            part = rs_src[p].reshape(2 * HD, T)
            sums.append(tn(ut[...], part)[p * RANK : (p + 1) * RANK])
        ups.scatter(ADAPTER_SCALE * jnp.concatenate(sums, axis=0))
        downs.reduce()

    def step_up2():
        ups.reduce()

    def step_rsy():
        @pl.when(own_in)
        def _():
            for p in (1, 0):
                drain(rsy.at[p, 0 : NY - 1], ryr.at[p])
                total = rsy[p, 0].astype(F32)
                for n in range(1, NY):
                    total = total + rsy[p, n].astype(F32)
                rsz[p] = total.astype(BF16)

            def send(m, _):
                to = y * (2 * NZ) + m
                rows = pl.ds(pl.multiple_of(16 * m, 16), 16)

                @pl.when(to != i)
                def _():
                    remote(rsz.at[:, rows, :], rs_dst.at[z], rzs, rzr, (b, to)).start()

                return 0

            lax.fori_loop(0, 2 * NZ, send, 0)
            rs_dst[z] = rsz[:, pl.ds(pl.multiple_of(16 * (2 * z + core), 16), 16), :]

    def step_rsz():
        by(own_in, rzr, rs_dst.at[0 : NZ - 1], rs_dst)
        total = rs_dst[0].astype(F32)
        for n in range(1, NZ):
            total = total + rs_dst[n].astype(F32)
        kvg[:, mine, :] = total.astype(BF16)

    def step_dp():
        up_sum = ups.result()
        down_half = downs.result().astype(BF16)
        high = up_sum.astype(BF16)
        rest = up_sum - high.astype(F32)
        middle = rest.astype(BF16)
        low = (rest - middle.astype(F32)).astype(BF16)
        split = jnp.concatenate([high, middle, low], axis=0)
        grads = nn(split, normed[...])
        grad_down = grads[0:48] + (grads[48:96] + grads[96:144])
        grad_query = nn(down_half[0:RANK], qall[i])
        grad_kv = [
            nt(down_half[(1 + p) * RANK : (2 + p) * RANK], kvg[p, mine, :]) for p in range(2)
        ]
        for d in range(8):
            for p in range(3):
                pay[8 * d + 2 * p : 8 * d + 2 * p + 2, :] = grad_down[
                    p * RANK + 2 * d : p * RANK + 2 * d + 2
                ]
            pay[8 * d + 6 : 8 * d + 8, 0:QC] = grad_query[2 * d : 2 * d + 2]
            for p in range(2):
                start = QC + p * 128
                pay[8 * d + 6 : 8 * d + 8, start : start + 16] = grad_kv[p][2 * d : 2 * d + 2]

        def send(k, _):
            to = (b + 1 + k) % ndp
            remote(
                pay.at[pl.ds(pl.multiple_of(8 * to, 8), 8), :], dp_in.at[b], dps, dpr, (to, i)
            ).start()
            return 0

        lax.fori_loop(0, ndp - 1, send, 0)
        dp_in[b] = pay[pl.ds(pl.multiple_of(8 * b, 8), 8), :]
        acc[...] += tn(high, adown[...].reshape(3 * RANK, NC))

    stores = [
        pltpu.make_async_copy(src, dst, osem.at[n])
        for n, (src, dst) in enumerate(((ob, out_i.at[0]), (od, out_d), (oq, out_q), (okv, out_kv)))
    ]

    def step_dpout():
        for n in (11, 12, 13):
            loads[n].wait()
        if ndp > 1:
            drain(dp_in.at[0 : ndp - 1], dpr)
        total = dp_in[0]
        for n in range(1, ndp):
            total = total + dp_in[n]
        tokens = float(ndp * T)
        for p in range(3):
            od[p] = accd[p] + total[2 * p : 2 * p + 2, :] / tokens
        oq[...] = accq[...] + ADAPTER_SCALE * total[6:8, 0:QC] / tokens
        for p in range(2):
            start = QC + p * 128
            okv[p] = acckv[p] + ADAPTER_SCALE * total[6:8, start : start + 16] / tokens
        for copy in stores[1:]:
            copy.start()

    def step_kv():
        def far_kv(k, _):
            slot = 2 * k + 1 - core
            drain(g_ref(slot, None), gr.at[slot])
            return 0

        lax.fori_loop(0, HALF, far_kv, 0)
        for p in range(2):
            acc[...] += lax.dot_general(
                kvg[p], wkv[p], (((0,), (1,)), ((), ())), preferred_element_type=F32
            )

    def step_w():
        drain(wq, wsem)
        for n in (14, 15):
            loads[n].wait()

    steps = {
        "first": step_first, "col": step_col, "spr": step_spr, "fwd": step_fwd,
        "gfwd": step_gfwd, "mm": step_mm, "up": step_up, "up2": step_up2,
        "rsy": step_rsy, "rsz": step_rsz, "dp": step_dp, "dpout": step_dpout, "kv": step_kv,
        "w": step_w,
    }
    for name, *rest in ORDER:
        steps[name](*rest)
    ob[...] = acc[...].astype(BF16)
    stores[0].start()

    for n in range(2):
        by(own_in, kvs.at[n], kt.at[0:240, :], kt)
        by(own_in, rys.at[n], rs_src.at[n, 0], rs_src.at[n])
    by(own_in, uts, ut.at[0:240, :], ut)

    @pl.when(own_in)
    def _():
        drain(rsz.at[:, 0:112, :], rzs)

    for n, (first, last, _) in enumerate(CHUNKS):
        drain(qall.at[0:15, pl.ds(first, last - first), :], qs.at[n])
    drain(qall.at[0:16], fs)
    drain(kvg.at[:, 0:240, :], gs.at[0])
    drain(kvg.at[:, 0:256, :], gs.at[1])
    downs.finish()
    ups.finish()
    if ndp > 1:
        drain(dp_in.at[0 : ndp - 1], dps)
    for copy in stores:
        copy.wait()


def hand_over(*refs):
    copies = [
        pltpu.make_async_copy(refs[n], refs[4 + n], refs[8].at[n]) for n in range(4)
    ]
    for copy in copies:
        copy.start()
    for copy in copies:
        copy.wait()


def per_device(
    ndp, normed, queries, keys, values, context_grad, segments, w_query, w_key, w_value,
    adapter_down, up_query, up_keyvalue, accum_down, accum_query, accum_keyvalue,
):
    tab, tabt = rotary_tables()
    keys_t = jnp.transpose(keys[0])
    values_t = jnp.transpose(values[0])
    vmem = pltpu.VMEM
    dma = pltpu.SemaphoreType.DMA
    scratch = [
        vmem((T, NC), BF16),
        vmem((T, QC), BF16),
        vmem((T, QC), BF16),
        vmem((1, T), jnp.int32),
        vmem((NT, NC, QC), BF16),
        vmem((2, NC, 512), BF16),
        vmem((3, RANK, NC), BF16),
        vmem((RANK, QC), BF16),
        vmem((2, RANK, 16), BF16),
        vmem(accum_down.shape, F32),
        vmem(accum_query.shape, F32),
        vmem(accum_keyvalue.shape, F32),
        vmem(tab.shape, F32),
        vmem(tabt.shape, F32),
        vmem((2, 16, T), BF16),
        vmem((2 * HD, T), BF16),
        vmem((2 * HD, T), BF16),
        vmem((16, 128), BF16),
        vmem((2 * HD, 128), BF16),
        vmem((2, 2, HD, T), BF16),
        vmem((2, NY, HD, T), BF16),
        vmem((2, HD, T), BF16),
        vmem((NZ, 2, 16, T), BF16),
        vmem((NT, T, QC), BF16),
        vmem((2, 512, T), BF16),
        vmem((2, 2, 48, 128), F32),
        vmem((2, NT, 8, 128), F32),
        vmem((2, 2, 48, 128), F32),
        vmem((64, NC), F32),
        vmem((8, 8, NC), F32),
        vmem((T, NC), F32),
        vmem((T, T), F32),
        vmem((T, NC), BF16),
        vmem(accum_down.shape, F32),
        vmem(accum_query.shape, F32),
        vmem(accum_keyvalue.shape, F32),
        dma((16,)), dma,
        dma((2,)), dma((2,)), dma, dma, dma((2,)), dma((2,)), dma, dma,
        dma((len(CHUNKS),)), dma((len(CHUNKS), NT)), dma, dma((NT,)), dma((2,)), dma((NT,)),
        dma((2,)), dma((2,)), dma((2,)), dma((2,)), dma, dma, dma((4,)),
    ]
    out_shape = (
        jax.ShapeDtypeStruct((1, T, NC), BF16),
        jax.ShapeDtypeStruct(accum_down.shape, F32),
        jax.ShapeDtypeStruct(accum_query.shape, F32),
        jax.ShapeDtypeStruct(accum_keyvalue.shape, F32),
    )
    results = pl.pallas_call(
        functools.partial(kernel, ndp),
        out_shape=out_shape,
        in_specs=[pl.BlockSpec(memory_space=pl.ANY)] * 17,
        out_specs=tuple(pl.BlockSpec(memory_space=pl.ANY) for _ in out_shape),
        scratch_shapes=scratch,
        compiler_params=pltpu.CompilerParams(
            collective_id=0, has_side_effects=True, vmem_limit_bytes=64 * 1024 * 1024
        ),
    )(
        normed, queries, keys_t, values_t, context_grad, segments, w_query, w_key, w_value,
        adapter_down, up_query, up_keyvalue, accum_down, accum_query, accum_keyvalue,
        jnp.asarray(tab), jnp.asarray(tabt),
    )
    return pl.pallas_call(
        hand_over,
        out_shape=out_shape,
        in_specs=[pl.BlockSpec(memory_space=pltpu.VMEM)] * 4,
        out_specs=tuple(pl.BlockSpec(memory_space=pl.ANY) for _ in out_shape),
        scratch_shapes=[dma((4,))],
        compiler_params=pltpu.CompilerParams(vmem_limit_bytes=64 * 1024 * 1024),
    )(*results)


def solution(mesh):
    in_specs = (
        P("dp", None, "tensor"),
        P("dp", None, "tensor"),
        P("dp", None, "tensor"),
        P("dp", None, "tensor"),
        P("dp", None, "tensor"),
        P("dp", None),
        P("tensor", None),
        P("tensor", None),
        P("tensor", None),
        P(None, None, "tensor"),
        P(None, "tensor"),
        P(None, None, "tensor"),
        P(None, "dp", "tensor"),
        P("dp", "tensor"),
        P(None, "dp", "tensor"),
    )
    out_specs = (
        P("dp", None, "tensor"),
        P(None, "dp", "tensor"),
        P("dp", "tensor"),
        P(None, "dp", "tensor"),
    )
    return jax.shard_map(
        functools.partial(per_device, mesh.shape["dp"]),
        mesh=mesh, in_specs=in_specs, out_specs=out_specs, check_vma=False,
    )
```

```python
import functools
import math

import jax
import jax.numpy as jnp
import numpy as np
from jax import lax
from jax.experimental import pallas as pl
from jax.experimental.pallas import tpu as pltpu
from jax.sharding import PartitionSpec as P

HD = 128
RANK = 16
ADAPTER_SCALE = 2.0
ROPE_BASE = 500000.0
F32 = jnp.float32
BF16 = jnp.bfloat16
MESH = pl.DeviceIdType.MESH

NY, NZ = 4, 4
NT = NY * NZ * 2
HALF = NT // 2
T = 256
QC = 256
NC = 512


def rotary_tables():
    exponent = np.arange(HD // 2, dtype=np.float32) * np.float32(2.0 / HD)
    frequency = (1.0 / np.float32(ROPE_BASE) ** exponent).astype(np.float32)
    wavelength = (2.0 * math.pi / frequency).astype(np.float32)
    blend = (8192.0 / wavelength - 1.0) / 3.0
    middle = (1.0 - blend) * frequency / 8.0 + blend * frequency
    scaled = np.where(
        wavelength < 2048.0, frequency, np.where(wavelength > 8192.0, frequency / 8.0, middle)
    ).astype(np.float32)
    angle = np.arange(T, dtype=np.float32)[:, None] * scaled[None, :]
    cosine = np.cos(angle).astype(np.float32)
    sine = np.sin(angle).astype(np.float32)
    rows = np.stack(
        [np.concatenate([cosine, cosine], 1), np.concatenate([sine, -sine], 1)]
    )
    cols = np.stack([cosine.T, sine.T])
    return rows, cols


def nt(left, right):
    return lax.dot_general(left, right, (((1,), (1,)), ((), ())), preferred_element_type=F32)


def nn(left, right):
    return lax.dot_general(left, right, (((1,), (0,)), ((), ())), preferred_element_type=F32)


def tn(left, right):
    return lax.dot_general(left, right, (((0,), (0,)), ((), ())), preferred_element_type=F32)


CHUNKS = ((0, 128, "z"), (128, 224, "z"), (224, 256, "y"))

FAR = (
    (2, 2), (2, 1), (2, -1), (1, 2), (-1, 2), (0, 2), (1, 1), (1, -1), (-1, 1), (-1, -1),
    (2, 0), (0, 1), (0, -1), (1, 0), (-1, 0), (0, 0),
)

ORDER = (
    ("first", 1), ("first", 2), ("up",), ("fwd", 0, 0), ("w",), ("mm", 0, 0), ("spr", 0, 0, 1),
    ("spr", 0, 0, -1), ("col", 0, 1), ("col", 0, -1), ("rsy", 1), ("col", 1, 1), ("col", 1, -1),
    ("rsy", 0), ("spr", 1, 0, 1), ("spr", 1, 0, -1), ("spr", 2, 0, 1), ("spr", 2, 0, -1),
    ("fwd", 0, 1), ("fwd", 0, -1), ("col", 2, 1), ("col", 2, -1), ("fwd", 1, 0), ("fwd", -1, 0),
    ("mm", 0, 1), ("mm", 0, -1), ("mm", 1, 0), ("col", 0, 2), ("mm", -1, 0), ("spr", 0, 1, 1),
    ("spr", 0, 1, -1), ("up2",), ("col", 1, 2), ("spr", 0, -1, 1), ("spr", 0, -1, -1),
    ("rsz", 1), ("gfirst", 1), ("fwd", 0, 2), ("spr", 1, 1, 1), ("spr", 1, 1, -1),
    ("spr", 2, 1, 1), ("spr", 2, 1, -1), ("fwd", 1, 1), ("rsz", 0), ("gfirst", 0),
    ("spr", 1, -1, 1), ("spr", 1, -1, -1), ("spr", 2, -1, 1), ("spr", 2, -1, -1),
    ("fwd", -1, 1), ("fwd", 1, -1), ("fwd", -1, -1), ("mm", 0, 2), ("col", 2, 2), ("fwd", 2, 0),
    ("mm", 1, 1), ("mm", -1, 1), ("gcol", 1, 1), ("gcol", 1, -1), ("spr", 0, 2, 1),
    ("spr", 0, 2, -1), ("mm", 1, -1), ("mm", -1, -1), ("mm", 2, 0), ("gcol", 0, 1),
    ("gcol", 0, -1), ("gcol", 1, 2), ("spr", 2, 2, 1), ("spr", 2, 2, -1), ("spr", 1, 2, 1),
    ("spr", 1, 2, -1), ("fwd", 1, 2), ("fwd", -1, 2), ("gcol", 0, 2), ("mm", 1, 2),
    ("fwd", 2, 1), ("mm", -1, 2), ("dp",), ("gfwd", 1, 0), ("fwd", 2, -1), ("mm", 2, 1),
    ("gfwd", 0, 0), ("mm", 2, -1), ("gfwd", 1, 1), ("gfwd", 1, -1), ("fwd", 2, 2),
    ("gfwd", 0, 1), ("gfwd", 0, -1), ("gfwd", 1, 2), ("mm", 2, 2), ("gfwd", 0, 2), ("kv", 1),
    ("kv", 0), ("dpout",),
)


def kernel(
    ndp,
    normed_h, queries_h, keys_h, values_h, cot_h, seg_h, wq_h, wk_h, wv_h,
    adown_h, upq_h, upkv_h, accd_h, accq_h, acckv_h, tab_h, tabt_h,
    out_i, out_d, out_q, out_kv,
    normed, queries, cot, seg, wq, wkv, adown, upq, upkv, accd, accq, acckv, tab, tabt,
    kvown, kt, vt, utown, ut, rs_src, rsy, rsz, rs_dst, qall, kvg, ps_src, ps_in, ps_all,
    pay, dp_in, acc, bias, ob, od, oq, okv,
    lsem, wsem, kvs, kvr, zs, zr, ys, yr, rys, ryr, rzs, rzr, qs, qr, fs, fr, gs, gr,
    pss, psr, pas, par, dps, dpr, osem,
):
    i = lax.axis_index("tensor")
    b = lax.axis_index("dp")
    core = i % 2
    z = (i // 2) % NZ
    y = i // (2 * NZ)
    side = i // HALF
    own_in = core == side

    def dev(dy, dz, dc):
        return (((y + dy) % NY) * NZ + (z + dz) % NZ) * 2 + (core + dc) % 2

    loads = [
        (keys_h, kvown.at[0]), (values_h, kvown.at[1]), (queries_h.at[0], queries),
        (cot_h.at[0], cot), (seg_h, seg), (normed_h.at[0], normed), (adown_h, adown),
        (upq_h, upq), (upkv_h, upkv), (tab_h, tab), (tabt_h, tabt),
        (accd_h, accd), (accq_h, accq), (acckv_h, acckv), (wk_h, wkv.at[0]), (wv_h, wkv.at[1]),
    ]
    loads = [pltpu.make_async_copy(src, dst, lsem.at[n]) for n, (src, dst) in enumerate(loads)]
    barrier = pltpu.get_barrier_semaphore()

    def greet_t(k, _):
        pl.semaphore_signal(
            barrier, 1, device_id=(b, (i + 1 + k) % NT), device_id_type=MESH
        )
        return 0

    def greet_d(k, _):
        pl.semaphore_signal(
            barrier, 1, device_id=((b + 1 + k) % ndp, i), device_id_type=MESH
        )
        return 0

    lax.fori_loop(0, NT - 1, greet_t, 0)
    lax.fori_loop(0, ndp - 1, greet_d, 0)
    for copy in loads:
        copy.start()

    def load_w(k, _):
        pltpu.make_async_copy(
            wq_h.at[:, pl.ds(pl.multiple_of(k * QC, QC), QC)], wq.at[k], wsem
        ).start()
        return 0

    def remote(src, dst, send, recv, to):
        return pltpu.make_async_remote_copy(
            src_ref=src, dst_ref=dst, send_sem=send, recv_sem=recv,
            device_id=to, device_id_type=MESH,
        )

    def drain(ref, sem):
        pltpu.make_async_copy(ref, ref, sem).wait()

    def by(test, sem, part, whole):
        @pl.when(test)
        def _():
            drain(part, sem)

        @pl.when(jnp.logical_not(test))
        def _():
            drain(whole, sem)

    owner = (i < 24) & (core == (i // 2) % 2)

    def piece(ref, n):
        return ref.at[n % 2, pl.ds(pl.multiple_of(16 * (n // 2), 16), 16), :]

    def scatter_sums():
        def send(k, _):
            n = (k % 3) * NZ + (z + 2 + k // 3) % NZ
            to = 2 * n + n % 2

            @pl.when(to != i)
            def _():
                remote(piece(ps_src, n), ps_in.at[i], pss, psr, (b, to)).start()

            return 0

        lax.fori_loop(0, 12, send, 0)

    def reduce_sums():
        @pl.when(owner)
        def _():
            n = i // 2
            rows = pl.ds(pl.multiple_of(16 * (n // 2), 16), 16)
            ps_in[i] = ps_src[n % 2, rows, :]
            drain(ps_in.at[0 : NT - 1], psr)
            ps_all[n % 2, rows, :] = jnp.sum(ps_in[...].astype(F32), axis=0).astype(BF16)

            def send(k, _):
                ref = piece(ps_all, n)
                remote(ref, ref, pas, par, (b, (i + 1 + k) % NT)).start()
                return 0

            lax.fori_loop(0, NT - 1, send, 0)

    loads[0].wait()
    loads[1].wait()
    loads[8].wait()
    rank = lax.broadcasted_iota(jnp.int32, (RANK, 128), 0)
    lane = lax.broadcasted_iota(jnp.int32, (RANK, 128), 1)
    columns = jnp.zeros((16, 128), F32)
    for p in range(2):
        place = jnp.where(lane == rank + p * RANK, 1.0, 0.0).astype(BF16)
        columns = columns + tn(upkv[p], place)
    utown[...] = columns.astype(BF16)
    pl.semaphore_wait(barrier, NT - 1 + ndp - 1)

    home = pl.ds(pl.multiple_of((i % HALF) * 16, 16), 16)

    def scatter_home(src, dst, send, recv, lanes=slice(None)):
        for dy, dz in FAR:
            to = dev(dy, dz, side - core)

            def start():
                remote(
                    src.at[:, lanes], dst.at[home, lanes], send, recv, (b, to)
                ).start()

            if (dy, dz) == (0, 0):
                pl.when(to != i)(start)
            else:
                start()

        @pl.when(own_in)
        def _():
            dst[home, lanes] = src[:, lanes]

    my_row = pl.ds(pl.multiple_of((y % 2) * HD, HD), HD)

    def along_z(src, dst, n, lanes):
        for dz in (2, 1, -1, 0):
            to = dev(0, dz, side - core)

            def start():
                remote(
                    src.at[:, lanes], dst.at[home, lanes], zs.at[n], zr.at[n], (b, to)
                ).start()

            if dz == 0:
                pl.when(to != i)(start)
            else:
                start()

        @pl.when(own_in)
        def _():
            dst[home, lanes] = src[:, lanes]

    def along_y(dst, n, lanes):
        @pl.when(own_in)
        def _():
            drain(dst.at[0:112, lanes], zr.at[n])
            for dy in (2, 1, -1):
                ref = dst.at[my_row, lanes]
                remote(ref, ref, ys.at[n], yr.at[n], (b, dev(dy, 0, 0))).start()

    early, late = slice(0, T // 2), slice(T // 2, T)
    along_z(kvown.at[1], vt, 0, late)
    along_z(utown, ut, 1, slice(None))
    scatter_home(kvown.at[0], kt, kvs.at[0], kvr.at[0], early)
    scatter_home(kvown.at[1], vt, kvs.at[1], kvr.at[1], early)
    scatter_home(kvown.at[0], kt, kvs.at[2], kvr.at[2], late)

    loads[5].wait()
    loads[6].wait()
    down_part = nt(adown[...].reshape(3 * RANK, NC), normed[...]).astype(BF16)
    for n in range(2):
        ps_src[n, 48:96, :] = down_part[:, n * 128 : (n + 1) * 128]
    loads[4].wait()
    doc = jnp.broadcast_to(seg[...].astype(F32), (T, T))
    row = lax.broadcasted_iota(jnp.int32, (T, T), 0)
    col = lax.broadcasted_iota(jnp.int32, (T, T), 1)
    bias[...] = jnp.where((col <= row) & (doc == doc.T), 0.0, -jnp.inf)
    acc[...] = jnp.zeros_like(acc)
    lax.fori_loop(0, NT, load_w, 0)
    for n in (2, 3, 7, 9, 10):
        loads[n].wait()

    class Gather:
        def __init__(self, axis, ref, send, recv):
            self.axis, self.ref, self.s, self.r = axis, ref, send, recv

        def at(self, d, e):
            return dev(e, d, 0) if self.axis == "z" else dev(d, e, 0)

        def push(self, slot, to, part=None):
            ref = self.ref(slot, part)
            remote(ref, ref, self.s, self.r.at[slot], (b, to)).start()

        def wait(self, slot):
            drain(self.ref(slot, None), self.r.at[slot])

        def first(self):
            for d, e in ((1, 0), (-1, 0), (0, 1), (0, -1)):
                self.push(i, self.at(d, e))

        def col(self, d):
            slot = self.at(d, 0)
            self.wait(slot)
            if d != 2:
                self.push(slot, self.at(-d, 0), 0 if d == -1 else 1)
            for e in (1, -1):
                self.push(slot, self.at(0, e))

        def spr(self, d, e):
            slot = self.at(d, e)
            self.wait(slot)
            self.push(slot, self.at(0, -e), 0 if e == -1 else 1)

        def far(self, dy, dz):
            if (dy if self.axis == "z" else dz) == 2:
                self.wait(dev(dy, dz, 0))

    def q_ref(first, last):
        half = (last - first) // 2

        def ref(slot, part):
            if part is None:
                return qall.at[slot, pl.ds(first, last - first), :]
            return qall.at[slot, pl.ds(first + part * half, half), :]

        return ref

    def g_ref(p, slot):
        return kvg.at[p, pl.ds(pl.multiple_of(slot * 16, 16), 16), :]

    gathers = {
        n: Gather(axis, q_ref(first, last), qs.at[n], qr.at[n])
        for n, (first, last, axis) in enumerate(CHUNKS)
    }
    mine = pl.ds(pl.multiple_of(i * 16, 16), 16)
    other = i + 1 - 2 * core

    def send_rsy(p, h):
        to = ((2 * core + h) * NZ + z) * 2 + core

        @pl.when(to != i)
        def _():
            remote(rs_src.at[p, h], rsy.at[p, y], rys.at[p], ryr.at[p], (b, to)).start()

        @pl.when(to == i)
        def _():
            rsy[p, y] = rs_src[p, h]

    def wait_home(n, ref, lanes):
        by(own_in, kvr.at[n], ref.at[0:240, lanes], ref.at[:, lanes])

    scale = 1.0 / math.sqrt(HD)
    heads = [slice(0, HD), slice(HD, 2 * HD)]
    cosine, sine = tabt[0], tabt[1]

    def softmax(h, rows, keys):
        scores = nn(queries[rows, h], kt[h, keys]) * scale + bias[rows, keys]
        weights = jnp.exp(scores - jnp.max(scores, axis=1, keepdims=True))
        return weights / jnp.sum(weights, axis=1, keepdims=True)

    def score_cotangent(h, rows, keys, weights):
        weight_grad = nn(cot[rows, h], vt[h, keys])
        delta = jnp.sum(weights * weight_grad, axis=1, keepdims=True)
        return (weights * (weight_grad - delta)).astype(BF16)

    def query_cotangent(h, rows, keys, score_grad):
        rot = nt(score_grad, kt[h, keys]) * scale
        qall[i, rows, h] = (
            rot * tab[0, rows, :] + pltpu.roll(rot, HD // 2, 1) * tab[1, rows, :]
        ).astype(BF16)

    def both(left, one, two):
        top = tn(left[early], one)
        rest = tn(left[late], two)
        return jnp.concatenate([rest[:, early] + top, rest[:, late]], axis=1)

    every = slice(0, T)
    wait_home(0, kt, early)
    along_y(vt, 0, late)
    along_y(ut, 1, slice(None))
    probs_early = [softmax(h, early, early) for h in heads]
    wait_home(1, vt, early)
    grads_early = []
    for n, h in enumerate(heads):
        grads_early.append(score_cotangent(h, early, early, probs_early[n]))
        query_cotangent(h, early, early, grads_early[n])
    gathers[0].first()
    wait_home(2, kt, late)
    probs = []
    for n, h in enumerate(heads):
        probs.append(softmax(h, late, every))
        rs_src[1, n] = both(
            cot[:, h], probs_early[n].astype(BF16), probs[n].astype(BF16)
        ).astype(BF16)
        send_rsy(1, n)
    by(own_in, yr.at[0], vt.at[0:HD, late], vt.at[:, late])
    grads = []
    for n, h in enumerate(heads):
        grads.append(score_cotangent(h, late, every, probs[n]))
        key_rot = both(queries[:, h], grads_early[n], grads[n]) * scale
        one, two = key_rot[: HD // 2], key_rot[HD // 2 :]
        rs_src[0, n] = jnp.concatenate(
            [one * cosine + two * sine, two * cosine - one * sine], axis=0
        ).astype(BF16)
        send_rsy(0, n)
    for n, h in enumerate(heads):
        query_cotangent(h, late, every, grads[n])

    def step_first(tag):
        gathers[tag].first()

    def step_col(tag, d):
        gathers[tag].col(d)

    def step_spr(tag, d, e):
        gathers[tag].spr(d, e)

    def step_fwd(dy, dz):
        slot = dev(dy, dz, 0)
        for n in range(len(CHUNKS)):
            gathers[n].far(dy, dz)
        remote(qall.at[slot], qall.at[slot], fs, fr.at[slot], (b, other)).start()

    def push_g(p, slot, to):
        ref = g_ref(p, slot)
        remote(ref, ref, gs.at[p], gr.at[p, slot], (b, to)).start()

    def wait_g(p, slot):
        drain(g_ref(p, slot), gr.at[p, slot])

    def step_gfirst(p):
        for dy, dz in ((0, 2), (0, 1), (0, -1), (2, 0), (1, 0), (-1, 0)):
            push_g(p, i, dev(dy, dz, 0))

    def step_gcol(p, dz):
        wait_g(p, dev(0, dz, 0))
        for dy in (2, 1, -1):
            push_g(p, dev(0, dz, 0), dev(dy, 0, 0))

    def step_gfwd(p, dz):
        for dy in (0, 1, -1, 2):
            slot = dev(dy, dz, 0)
            if dy != 0:
                wait_g(p, slot)
            ref = g_ref(p, slot)
            remote(ref, ref, gs.at[2 + p], gr.at[p, slot], (b, other)).start()

    def step_mm(dy, dz):
        one, two = dev(dy, dz, 0), dev(dy, dz, 1)
        drain(qall.at[two], fr.at[two])
        acc[...] += nt(qall[one], wq[one]) + nt(qall[two], wq[two])

    def step_up():
        by(own_in, yr.at[1], ut.at[0:HD, :], ut)
        sums = [nt(upq[...], qall[i])]
        for p in range(2):
            part = rs_src[p].reshape(2 * HD, T)
            sums.append(tn(ut[...], part)[p * RANK : (p + 1) * RANK])
        up_part = (ADAPTER_SCALE * jnp.concatenate(sums, axis=0)).astype(BF16)
        for n in range(2):
            ps_src[n, 0:48, :] = up_part[:, n * 128 : (n + 1) * 128]
        scatter_sums()

    def step_up2():
        reduce_sums()

    def step_rsy(p):
        @pl.when(own_in)
        def _():
            drain(rsy.at[p, 0 : NY - 1], ryr.at[p])
            total = rsy[p, 0].astype(F32)
            for n in range(1, NY):
                total = total + rsy[p, n].astype(F32)
            rsz[p] = total.astype(BF16)
            for dz in (2, 1, -1, 0):
                for dc in range(2):
                    to = dev(0, dz, dc)
                    rows = pl.ds(pl.multiple_of(16 * (to % (2 * NZ)), 16), 16)
                    if (dz, dc) == (0, 0):
                        rs_dst[p, z] = rsz[p, rows, :]
                    else:
                        remote(
                            rsz.at[p, rows, :], rs_dst.at[p, z], rzs.at[p], rzr.at[p], (b, to)
                        ).start()

    def step_rsz(p):
        by(own_in, rzr.at[p], rs_dst.at[p, 0 : NZ - 1], rs_dst.at[p])
        total = rs_dst[p, 0].astype(F32)
        for n in range(1, NZ):
            total = total + rs_dst[p, n].astype(F32)
        kvg[p, mine, :] = total.astype(BF16)

    def step_dp():
        by(owner, par, ps_in.at[0:11], ps_in.at[0:12])
        sums = jnp.concatenate([ps_all[0], ps_all[1]], axis=1)
        up_half, down_half = sums[0:48], sums[48:96]
        grad_down = nn(up_half, normed[...])
        grad_query = nn(down_half[0:RANK], qall[i])
        grad_kv = [
            nt(down_half[(1 + p) * RANK : (2 + p) * RANK], kvg[p, mine, :]) for p in range(2)
        ]
        for d in range(8):
            for p in range(3):
                pay[8 * d + 2 * p : 8 * d + 2 * p + 2, :] = grad_down[
                    p * RANK + 2 * d : p * RANK + 2 * d + 2
                ]
            pay[8 * d + 6 : 8 * d + 8, 0:QC] = grad_query[2 * d : 2 * d + 2]
            for p in range(2):
                start = QC + p * 128
                pay[8 * d + 6 : 8 * d + 8, start : start + 16] = grad_kv[p][2 * d : 2 * d + 2]

        def send(k, _):
            to = (b + 1 + k) % ndp
            remote(
                pay.at[pl.ds(pl.multiple_of(8 * to, 8), 8), :], dp_in.at[b], dps, dpr, (to, i)
            ).start()
            return 0

        lax.fori_loop(0, ndp - 1, send, 0)
        dp_in[b] = pay[pl.ds(pl.multiple_of(8 * b, 8), 8), :]
        acc[...] += tn(up_half, adown[...].reshape(3 * RANK, NC))

    stores = [
        pltpu.make_async_copy(src, dst, osem.at[n])
        for n, (src, dst) in enumerate(((ob, out_i.at[0]), (od, out_d), (oq, out_q), (okv, out_kv)))
    ]

    def step_dpout():
        for n in (11, 12, 13):
            loads[n].wait()
        if ndp > 1:
            drain(dp_in.at[0 : ndp - 1], dpr)
        total = dp_in[0]
        for n in range(1, ndp):
            total = total + dp_in[n]
        tokens = float(ndp * T)
        for p in range(3):
            od[p] = accd[p] + total[2 * p : 2 * p + 2, :] / tokens
        oq[...] = accq[...] + ADAPTER_SCALE * total[6:8, 0:QC] / tokens
        for p in range(2):
            start = QC + p * 128
            okv[p] = acckv[p] + ADAPTER_SCALE * total[6:8, start : start + 16] / tokens
        for copy in stores[1:]:
            copy.start()

    def step_kv(p):
        def far_kv(k, _):
            wait_g(p, 2 * k + 1 - core)
            return 0

        lax.fori_loop(0, HALF, far_kv, 0)
        acc[...] += lax.dot_general(
            kvg[p], wkv[p], (((0,), (1,)), ((), ())), preferred_element_type=F32
        )

    def step_w():
        drain(wq, wsem)
        for n in (14, 15):
            loads[n].wait()

    steps = {
        "first": step_first, "col": step_col, "spr": step_spr, "fwd": step_fwd,
        "gfirst": step_gfirst, "gcol": step_gcol, "gfwd": step_gfwd, "mm": step_mm, "up": step_up, "up2": step_up2,
        "rsy": step_rsy, "rsz": step_rsz, "dp": step_dp, "dpout": step_dpout, "kv": step_kv,
        "w": step_w,
    }
    for name, *rest in ORDER:
        steps[name](*rest)
    ob[...] = acc[...].astype(BF16)
    stores[0].start()

    for n in range(3):
        by(own_in, kvs.at[n], kt.at[0:240, early], kt.at[:, early])
    for n, lanes in enumerate((late, slice(None))):
        ref = (vt, ut)[n]
        by(own_in, zs.at[n], ref.at[0:48, lanes], ref.at[0:64, lanes])

        @pl.when(own_in)
        def _():
            drain(qall.at[0, 0:192, :], ys.at[n])

    for p in range(2):
        by(own_in, rys.at[p], rs_src.at[p, 0], rs_src.at[p])

        @pl.when(own_in)
        def _():
            drain(rsz.at[p, 0:112, :], rzs.at[p])

        drain(kvg.at[p, 0:240, :], gs.at[p])
        drain(kvg.at[p, 0:256, :], gs.at[2 + p])
    for n, (first, last, _) in enumerate(CHUNKS):
        drain(qall.at[0:15, pl.ds(first, last - first), :], qs.at[n])
    drain(qall.at[0:16], fs)
    by(owner, pss, ps_in.at[0:11], ps_in.at[0:12])

    @pl.when(owner)
    def _():
        drain(ps_in.at[0 : NT - 1], pas)

    if ndp > 1:
        drain(dp_in.at[0 : ndp - 1], dps)
    for copy in stores:
        copy.wait()


def hand_over(*refs):
    copies = [
        pltpu.make_async_copy(refs[n], refs[4 + n], refs[8].at[n]) for n in range(4)
    ]
    for copy in copies:
        copy.start()
    for copy in copies:
        copy.wait()


def per_device(
    ndp, normed, queries, keys, values, context_grad, segments, w_query, w_key, w_value,
    adapter_down, up_query, up_keyvalue, accum_down, accum_query, accum_keyvalue,
):
    tab, tabt = rotary_tables()
    keys_t = jnp.transpose(keys[0])
    values_t = jnp.transpose(values[0])
    vmem = pltpu.VMEM
    dma = pltpu.SemaphoreType.DMA
    scratch = [
        vmem((T, NC), BF16),
        vmem((T, QC), BF16),
        vmem((T, QC), BF16),
        vmem((1, T), jnp.int32),
        vmem((NT, NC, QC), BF16),
        vmem((2, NC, 512), BF16),
        vmem((3, RANK, NC), BF16),
        vmem((RANK, QC), BF16),
        vmem((2, RANK, 16), BF16),
        vmem(accum_down.shape, F32),
        vmem(accum_query.shape, F32),
        vmem(accum_keyvalue.shape, F32),
        vmem(tab.shape, F32),
        vmem(tabt.shape, F32),
        vmem((2, 16, T), BF16),
        vmem((2 * HD, T), BF16),
        vmem((2 * HD, T), BF16),
        vmem((16, 128), BF16),
        vmem((2 * HD, 128), BF16),
        vmem((2, 2, HD, T), BF16),
        vmem((2, NY, HD, T), BF16),
        vmem((2, HD, T), BF16),
        vmem((2, NZ, 16, T), BF16),
        vmem((NT, T, QC), BF16),
        vmem((2, 512, T), BF16),
        vmem((2, 96, 128), BF16),
        vmem((NT, 16, 128), BF16),
        vmem((2, 96, 128), BF16),
        vmem((64, NC), F32),
        vmem((8, 8, NC), F32),
        vmem((T, NC), F32),
        vmem((T, T), F32),
        vmem((T, NC), BF16),
        vmem(accum_down.shape, F32),
        vmem(accum_query.shape, F32),
        vmem(accum_keyvalue.shape, F32),
        dma((16,)), dma,
        dma((3,)), dma((3,)), dma((2,)), dma((2,)), dma((2,)), dma((2,)),
        dma((2,)), dma((2,)), dma((2,)), dma((2,)),
        dma((len(CHUNKS),)), dma((len(CHUNKS), NT)), dma, dma((NT,)), dma((4,)), dma((2, NT)),
        dma, dma, dma, dma, dma, dma, dma((4,)),
    ]
    out_shape = (
        jax.ShapeDtypeStruct((1, T, NC), BF16),
        jax.ShapeDtypeStruct(accum_down.shape, F32),
        jax.ShapeDtypeStruct(accum_query.shape, F32),
        jax.ShapeDtypeStruct(accum_keyvalue.shape, F32),
    )
    results = pl.pallas_call(
        functools.partial(kernel, ndp),
        out_shape=out_shape,
        in_specs=[pl.BlockSpec(memory_space=pl.ANY)] * 17,
        out_specs=tuple(pl.BlockSpec(memory_space=pl.ANY) for _ in out_shape),
        scratch_shapes=scratch,
        compiler_params=pltpu.CompilerParams(
            collective_id=0, has_side_effects=True, vmem_limit_bytes=64 * 1024 * 1024
        ),
    )(
        normed, queries, keys_t, values_t, context_grad, segments, w_query, w_key, w_value,
        adapter_down, up_query, up_keyvalue, accum_down, accum_query, accum_keyvalue,
        jnp.asarray(tab), jnp.asarray(tabt),
    )
    return pl.pallas_call(
        hand_over,
        out_shape=out_shape,
        in_specs=[pl.BlockSpec(memory_space=pltpu.VMEM)] * 4,
        out_specs=tuple(pl.BlockSpec(memory_space=pl.ANY) for _ in out_shape),
        scratch_shapes=[dma((4,))],
        compiler_params=pltpu.CompilerParams(vmem_limit_bytes=64 * 1024 * 1024),
    )(*results)


def solution(mesh):
    in_specs = (
        P("dp", None, "tensor"),
        P("dp", None, "tensor"),
        P("dp", None, "tensor"),
        P("dp", None, "tensor"),
        P("dp", None, "tensor"),
        P("dp", None),
        P("tensor", None),
        P("tensor", None),
        P("tensor", None),
        P(None, None, "tensor"),
        P(None, "tensor"),
        P(None, None, "tensor"),
        P(None, "dp", "tensor"),
        P("dp", "tensor"),
        P(None, "dp", "tensor"),
    )
    out_specs = (
        P("dp", None, "tensor"),
        P(None, "dp", "tensor"),
        P("dp", "tensor"),
        P(None, "dp", "tensor"),
    )
    return jax.shard_map(
        functools.partial(per_device, mesh.shape["dp"]),
        mesh=mesh, in_specs=in_specs, out_specs=out_specs, check_vma=False,
    )
```

```python
import functools
import math

import jax
import jax.numpy as jnp
import numpy as np
from jax import lax
from jax.experimental import pallas as pl
from jax.experimental.pallas import tpu as pltpu
from jax.sharding import PartitionSpec as P

HD = 128
RANK = 16
ADAPTER_SCALE = 2.0
ROPE_BASE = 500000.0
F32 = jnp.float32
BF16 = jnp.bfloat16
MESH = pl.DeviceIdType.MESH

NY, NZ = 4, 4
NT = NY * NZ * 2
HALF = NT // 2
T = 256
QC = 256
NC = 512


def rotary_tables():
    exponent = np.arange(HD // 2, dtype=np.float32) * np.float32(2.0 / HD)
    frequency = (1.0 / np.float32(ROPE_BASE) ** exponent).astype(np.float32)
    wavelength = (2.0 * math.pi / frequency).astype(np.float32)
    blend = (8192.0 / wavelength - 1.0) / 3.0
    middle = (1.0 - blend) * frequency / 8.0 + blend * frequency
    scaled = np.where(
        wavelength < 2048.0, frequency, np.where(wavelength > 8192.0, frequency / 8.0, middle)
    ).astype(np.float32)
    angle = np.arange(T, dtype=np.float32)[:, None] * scaled[None, :]
    cosine = np.cos(angle).astype(np.float32)
    sine = np.sin(angle).astype(np.float32)
    rows = np.stack(
        [np.concatenate([cosine, cosine], 1), np.concatenate([sine, -sine], 1)]
    )
    cols = np.stack([cosine.T, sine.T])
    return rows, cols


def nt(left, right):
    return lax.dot_general(left, right, (((1,), (1,)), ((), ())), preferred_element_type=F32)


def nn(left, right):
    return lax.dot_general(left, right, (((1,), (0,)), ((), ())), preferred_element_type=F32)


def tn(left, right):
    return lax.dot_general(left, right, (((0,), (0,)), ((), ())), preferred_element_type=F32)


CHUNKS = ((0, 128, "z"), (128, 224, "z"), (224, 256, "y"))

FAR = (
    (2, 2), (2, 1), (2, -1), (1, 2), (-1, 2), (0, 2), (1, 1), (1, -1), (-1, 1), (-1, -1),
    (2, 0), (0, 1), (0, -1), (1, 0), (-1, 0), (0, 0),
)

ORDER = (
    ("first", 1), ("first", 2), ("up",), ("fwd", 0, 0), ("w",), ("mm", 0, 0), ("spr", 0, 0, 1),
    ("spr", 0, 0, -1), ("col", 0, 1), ("col", 0, -1), ("rsy", 1), ("col", 1, 1), ("col", 1, -1),
    ("rsy", 0), ("spr", 1, 0, 1), ("spr", 1, 0, -1), ("spr", 2, 0, 1), ("spr", 2, 0, -1),
    ("fwd", 0, 1), ("fwd", 0, -1), ("col", 2, 1), ("col", 2, -1), ("fwd", 1, 0), ("fwd", -1, 0),
    ("mm", 0, 1), ("mm", 0, -1), ("mm", 1, 0), ("col", 0, 2), ("mm", -1, 0), ("spr", 0, 1, 1),
    ("spr", 0, 1, -1), ("up2",), ("col", 1, 2), ("spr", 0, -1, 1), ("spr", 0, -1, -1),
    ("rsz", 1), ("gfirst", 1), ("fwd", 0, 2), ("spr", 1, 1, 1), ("spr", 1, 1, -1),
    ("spr", 2, 1, 1), ("spr", 2, 1, -1), ("fwd", 1, 1), ("rsz", 0), ("gfirst", 0),
    ("spr", 1, -1, 1), ("spr", 1, -1, -1), ("spr", 2, -1, 1), ("spr", 2, -1, -1),
    ("fwd", -1, 1), ("fwd", 1, -1), ("fwd", -1, -1), ("mm", 0, 2), ("col", 2, 2), ("fwd", 2, 0),
    ("mm", 1, 1), ("mm", -1, 1), ("gcol", 1, 1), ("gcol", 1, -1), ("spr", 0, 2, 1),
    ("spr", 0, 2, -1), ("mm", 1, -1), ("mm", -1, -1), ("mm", 2, 0), ("gcol", 0, 1),
    ("gcol", 0, -1), ("gcol", 1, 2), ("spr", 2, 2, 1), ("spr", 2, 2, -1), ("spr", 1, 2, 1),
    ("spr", 1, 2, -1), ("fwd", 1, 2), ("fwd", -1, 2), ("gcol", 0, 2), ("mm", 1, 2),
    ("fwd", 2, 1), ("mm", -1, 2), ("dp",), ("gfwd", 1, 0), ("fwd", 2, -1), ("mm", 2, 1),
    ("gfwd", 0, 0), ("mm", 2, -1), ("gfwd", 1, 1), ("gfwd", 1, -1), ("fwd", 2, 2),
    ("gfwd", 0, 1), ("gfwd", 0, -1), ("gfwd", 1, 2), ("mm", 2, 2), ("gfwd", 0, 2), ("kv", 1),
    ("kv", 0), ("dpout",),
)


def kernel(
    ndp,
    normed_h, queries_h, keys_h, values_h, cot_h, seg_h, wq_h, wk_h, wv_h,
    adown_h, upq_h, upkv_h, accd_h, accq_h, acckv_h, tab_h, tabt_h,
    out_i, out_d, out_q, out_kv,
    normed, queries, cot, seg, wq, wkv, adown, upq, upkv, accd, accq, acckv, tab, tabt,
    kvown, kt, vt, utown, ut, rs_src, rsy, rsz, rs_dst, qall, kvg, ps_src, ps_in, ps_all,
    pay, dp_in, acc, bias,
    lsem, wsem, kvs, kvr, zs, zr, ys, yr, rys, ryr, rzs, rzr, qs, qr, fs, fr, gs, gr,
    pss, psr, pas, par, dps, dpr,
):
    i = lax.axis_index("tensor")
    b = lax.axis_index("dp")
    core = i % 2
    z = (i // 2) % NZ
    y = i // (2 * NZ)
    side = i // HALF
    own_in = core == side

    def dev(dy, dz, dc):
        return (((y + dy) % NY) * NZ + (z + dz) % NZ) * 2 + (core + dc) % 2

    loads = [
        (keys_h, kvown.at[0]), (values_h, kvown.at[1]), (queries_h.at[0], queries),
        (cot_h.at[0], cot), (seg_h, seg), (normed_h.at[0], normed), (adown_h, adown),
        (upq_h, upq), (upkv_h, upkv), (tab_h, tab), (tabt_h, tabt),
        (accd_h, accd), (accq_h, accq), (acckv_h, acckv), (wk_h, wkv.at[0]), (wv_h, wkv.at[1]),
    ]
    loads = [pltpu.make_async_copy(src, dst, lsem.at[n]) for n, (src, dst) in enumerate(loads)]
    barrier = pltpu.get_barrier_semaphore()

    def greet(to):
        pl.semaphore_signal(barrier, 1, device_id=to, device_id_type=MESH)

    def greet_d(k, _):
        greet(((b + 1 + k) % ndp, i))
        return 0

    for copy in loads[:2]:
        copy.start()
    for n, (dy, dz) in enumerate(FAR):
        for dc in (1, 0):
            if (dy, dz, dc) != (0, 0, 0):
                greet((b, dev(dy, dz, dc)))
        if n == 6:
            lax.fori_loop(0, ndp - 1, greet_d, 0)
    for copy in loads[2:]:
        copy.start()

    def load_w(k, _):
        pltpu.make_async_copy(
            wq_h.at[:, pl.ds(pl.multiple_of(k * QC, QC), QC)], wq.at[k], wsem
        ).start()
        return 0

    def remote(src, dst, send, recv, to):
        return pltpu.make_async_remote_copy(
            src_ref=src, dst_ref=dst, send_sem=send, recv_sem=recv,
            device_id=to, device_id_type=MESH,
        )

    def drain(ref, sem):
        pltpu.make_async_copy(ref, ref, sem).wait()

    def by(test, sem, part, whole):
        @pl.when(test)
        def _():
            drain(part, sem)

        @pl.when(jnp.logical_not(test))
        def _():
            drain(whole, sem)

    owner = (i < 24) & (core == (i // 2) % 2)

    def piece(ref, n):
        return ref.at[n % 2, pl.ds(pl.multiple_of(16 * (n // 2), 16), 16), :]

    def scatter_sums():
        def send(k, _):
            n = (k % 3) * NZ + (z + 2 + k // 3) % NZ
            to = 2 * n + n % 2

            @pl.when(to != i)
            def _():
                remote(piece(ps_src, n), ps_in.at[i], pss, psr, (b, to)).start()

            return 0

        lax.fori_loop(0, 12, send, 0)

    def reduce_sums():
        @pl.when(owner)
        def _():
            n = i // 2
            rows = pl.ds(pl.multiple_of(16 * (n // 2), 16), 16)
            ps_in[i] = ps_src[n % 2, rows, :]
            drain(ps_in.at[0 : NT - 1], psr)
            ps_all[n % 2, rows, :] = jnp.sum(ps_in[...].astype(F32), axis=0).astype(BF16)

            def send(k, _):
                ref = piece(ps_all, n)
                remote(ref, ref, pas, par, (b, (i + 1 + k) % NT)).start()
                return 0

            lax.fori_loop(0, NT - 1, send, 0)

    loads[0].wait()
    loads[1].wait()
    pl.semaphore_wait(barrier, NT - 1 + ndp - 1)

    home = pl.ds(pl.multiple_of((i % HALF) * 16, 16), 16)

    def scatter_home(src, dst, send, recv, lanes=slice(None)):
        for dy, dz in FAR:
            to = dev(dy, dz, side - core)

            def start():
                remote(
                    src.at[:, lanes], dst.at[home, lanes], send, recv, (b, to)
                ).start()

            if (dy, dz) == (0, 0):
                pl.when(to != i)(start)
            else:
                start()

        @pl.when(own_in)
        def _():
            dst[home, lanes] = src[:, lanes]

    my_row = pl.ds(pl.multiple_of((y % 2) * HD, HD), HD)

    def along_z(src, dst, n, lanes):
        for dz in (2, 1, -1, 0):
            to = dev(0, dz, side - core)

            def start():
                remote(
                    src.at[:, lanes], dst.at[home, lanes], zs.at[n], zr.at[n], (b, to)
                ).start()

            if dz == 0:
                pl.when(to != i)(start)
            else:
                start()

        @pl.when(own_in)
        def _():
            dst[home, lanes] = src[:, lanes]

    def along_y(dst, n, lanes):
        @pl.when(own_in)
        def _():
            drain(dst.at[0:112, lanes], zr.at[n])
            for dy in (2, 1, -1):
                ref = dst.at[my_row, lanes]
                remote(ref, ref, ys.at[n], yr.at[n], (b, dev(dy, 0, 0))).start()

    early, late = slice(0, T // 2), slice(T // 2, T)
    along_z(kvown.at[1], vt, 0, late)
    scatter_home(kvown.at[0], kt, kvs.at[0], kvr.at[0], early)
    scatter_home(kvown.at[1], vt, kvs.at[1], kvr.at[1], early)
    scatter_home(kvown.at[0], kt, kvs.at[2], kvr.at[2], late)
    loads[8].wait()
    rank = lax.broadcasted_iota(jnp.int32, (RANK, 128), 0)
    lane = lax.broadcasted_iota(jnp.int32, (RANK, 128), 1)
    columns = jnp.zeros((16, 128), F32)
    for p in range(2):
        place = jnp.where(lane == rank + p * RANK, 1.0, 0.0).astype(BF16)
        columns = columns + tn(upkv[p], place)
    utown[...] = columns.astype(BF16)
    along_z(utown, ut, 1, slice(None))

    loads[5].wait()
    loads[6].wait()
    down_part = nt(adown[...].reshape(3 * RANK, NC), normed[...]).astype(BF16)
    for n in range(2):
        ps_src[n, 48:96, :] = down_part[:, n * 128 : (n + 1) * 128]
    loads[4].wait()
    doc = jnp.broadcast_to(seg[...].astype(F32), (T, T))
    row = lax.broadcasted_iota(jnp.int32, (T, T), 0)
    col = lax.broadcasted_iota(jnp.int32, (T, T), 1)
    bias[...] = jnp.where((col <= row) & (doc == doc.T), 0.0, -jnp.inf)
    acc[...] = jnp.zeros_like(acc)
    for n in (2, 3, 7, 9, 10):
        loads[n].wait()

    class Gather:
        def __init__(self, axis, ref, send, recv):
            self.axis, self.ref, self.s, self.r = axis, ref, send, recv

        def at(self, d, e):
            return dev(e, d, 0) if self.axis == "z" else dev(d, e, 0)

        def push(self, slot, to, part=None):
            ref = self.ref(slot, part)
            remote(ref, ref, self.s, self.r.at[slot], (b, to)).start()

        def wait(self, slot):
            drain(self.ref(slot, None), self.r.at[slot])

        def first(self):
            for d, e in ((1, 0), (-1, 0), (0, 1), (0, -1)):
                self.push(i, self.at(d, e))

        def col(self, d):
            slot = self.at(d, 0)
            self.wait(slot)
            if d != 2:
                self.push(slot, self.at(-d, 0), 0 if d == -1 else 1)
            for e in (1, -1):
                self.push(slot, self.at(0, e))

        def spr(self, d, e):
            slot = self.at(d, e)
            self.wait(slot)
            self.push(slot, self.at(0, -e), 0 if e == -1 else 1)

        def far(self, dy, dz):
            if (dy if self.axis == "z" else dz) == 2:
                self.wait(dev(dy, dz, 0))

    def q_ref(first, last):
        half = (last - first) // 2

        def ref(slot, part):
            if part is None:
                return qall.at[slot, pl.ds(first, last - first), :]
            return qall.at[slot, pl.ds(first + part * half, half), :]

        return ref

    def g_ref(p, slot):
        return kvg.at[p, pl.ds(pl.multiple_of(slot * 16, 16), 16), :]

    gathers = {
        n: Gather(axis, q_ref(first, last), qs.at[n], qr.at[n])
        for n, (first, last, axis) in enumerate(CHUNKS)
    }
    mine = pl.ds(pl.multiple_of(i * 16, 16), 16)
    other = i + 1 - 2 * core

    def send_rsy(p, h):
        to = ((2 * core + h) * NZ + z) * 2 + core

        @pl.when(to != i)
        def _():
            remote(rs_src.at[p, h], rsy.at[p, y], rys.at[p], ryr.at[p], (b, to)).start()

        @pl.when(to == i)
        def _():
            rsy[p, y] = rs_src[p, h]

    def wait_home(n, ref, lanes):
        by(own_in, kvr.at[n], ref.at[0:240, lanes], ref.at[:, lanes])

    scale = 1.0 / math.sqrt(HD)
    heads = [slice(0, HD), slice(HD, 2 * HD)]
    cosine, sine = tabt[0], tabt[1]

    def softmax(h, rows, keys):
        scores = nn(queries[rows, h], kt[h, keys]) * scale + bias[rows, keys]
        weights = jnp.exp(scores - jnp.max(scores, axis=1, keepdims=True))
        return weights / jnp.sum(weights, axis=1, keepdims=True)

    def score_cotangent(h, rows, keys, weights):
        weight_grad = nn(cot[rows, h], vt[h, keys])
        delta = jnp.sum(weights * weight_grad, axis=1, keepdims=True)
        return (weights * (weight_grad - delta)).astype(BF16)

    def query_cotangent(h, rows, keys, score_grad):
        rot = nt(score_grad, kt[h, keys]) * scale
        qall[i, rows, h] = (
            rot * tab[0, rows, :] + pltpu.roll(rot, HD // 2, 1) * tab[1, rows, :]
        ).astype(BF16)

    def both(left, one, two):
        top = tn(left[early], one)
        rest = tn(left[late], two)
        return jnp.concatenate([rest[:, early] + top, rest[:, late]], axis=1)

    every = slice(0, T)
    wait_home(0, kt, early)
    along_y(vt, 0, late)
    probs_early = [softmax(h, early, early) for h in heads]
    wait_home(1, vt, early)
    grads_early = []
    for n, h in enumerate(heads):
        grads_early.append(score_cotangent(h, early, early, probs_early[n]))
        query_cotangent(h, early, early, grads_early[n])
    gathers[0].first()
    along_y(ut, 1, slice(None))
    wait_home(2, kt, late)
    probs = []
    for n, h in enumerate(heads):
        probs.append(softmax(h, late, every))
        rs_src[1, n] = both(
            cot[:, h], probs_early[n].astype(BF16), probs[n].astype(BF16)
        ).astype(BF16)
        send_rsy(1, n)
    by(own_in, yr.at[0], vt.at[0:HD, late], vt.at[:, late])
    grads = []
    for n, h in enumerate(heads):
        grads.append(score_cotangent(h, late, every, probs[n]))
        key_rot = both(queries[:, h], grads_early[n], grads[n]) * scale
        one, two = key_rot[: HD // 2], key_rot[HD // 2 :]
        rs_src[0, n] = jnp.concatenate(
            [one * cosine + two * sine, two * cosine - one * sine], axis=0
        ).astype(BF16)
        send_rsy(0, n)
    for n, h in enumerate(heads):
        query_cotangent(h, late, every, grads[n])
    lax.fori_loop(0, NT, load_w, 0)

    def step_first(tag):
        gathers[tag].first()

    def step_col(tag, d):
        gathers[tag].col(d)

    def step_spr(tag, d, e):
        gathers[tag].spr(d, e)

    def step_fwd(dy, dz):
        slot = dev(dy, dz, 0)
        for n in range(len(CHUNKS)):
            gathers[n].far(dy, dz)
        remote(qall.at[slot], qall.at[slot], fs, fr.at[slot], (b, other)).start()

    def push_g(p, slot, to):
        ref = g_ref(p, slot)
        remote(ref, ref, gs.at[p], gr.at[p, slot], (b, to)).start()

    def wait_g(p, slot):
        drain(g_ref(p, slot), gr.at[p, slot])

    def step_gfirst(p):
        for dy, dz in ((0, 2), (0, 1), (0, -1), (2, 0), (1, 0), (-1, 0)):
            push_g(p, i, dev(dy, dz, 0))

    def step_gcol(p, dz):
        wait_g(p, dev(0, dz, 0))
        for dy in (2, 1, -1):
            push_g(p, dev(0, dz, 0), dev(dy, 0, 0))

    def step_gfwd(p, dz):
        for dy in (0, 1, -1, 2):
            slot = dev(dy, dz, 0)
            if dy != 0:
                wait_g(p, slot)
            ref = g_ref(p, slot)
            remote(ref, ref, gs.at[2 + p], gr.at[p, slot], (b, other)).start()

    def step_mm(dy, dz):
        one, two = dev(dy, dz, 0), dev(dy, dz, 1)
        drain(qall.at[two], fr.at[two])
        acc[...] += nt(qall[one], wq[one]) + nt(qall[two], wq[two])

    def step_up():
        by(own_in, yr.at[1], ut.at[0:HD, :], ut)
        sums = [nt(upq[...], qall[i])]
        for p in range(2):
            part = rs_src[p].reshape(2 * HD, T)
            sums.append(tn(ut[...], part)[p * RANK : (p + 1) * RANK])
        up_part = (ADAPTER_SCALE * jnp.concatenate(sums, axis=0)).astype(BF16)
        for n in range(2):
            ps_src[n, 0:48, :] = up_part[:, n * 128 : (n + 1) * 128]
        scatter_sums()

    def step_up2():
        reduce_sums()

    def step_rsy(p):
        @pl.when(own_in)
        def _():
            drain(rsy.at[p, 0 : NY - 1], ryr.at[p])
            total = rsy[p, 0].astype(F32)
            for n in range(1, NY):
                total = total + rsy[p, n].astype(F32)
            rsz[p] = total.astype(BF16)
            for dz in (2, 1, -1, 0):
                for dc in range(2):
                    to = dev(0, dz, dc)
                    rows = pl.ds(pl.multiple_of(16 * (to % (2 * NZ)), 16), 16)
                    if (dz, dc) == (0, 0):
                        rs_dst[p, z] = rsz[p, rows, :]
                    else:
                        remote(
                            rsz.at[p, rows, :], rs_dst.at[p, z], rzs.at[p], rzr.at[p], (b, to)
                        ).start()

    def step_rsz(p):
        by(own_in, rzr.at[p], rs_dst.at[p, 0 : NZ - 1], rs_dst.at[p])
        total = rs_dst[p, 0].astype(F32)
        for n in range(1, NZ):
            total = total + rs_dst[p, n].astype(F32)
        kvg[p, mine, :] = total.astype(BF16)

    def step_dp():
        by(owner, par, ps_in.at[0:11], ps_in.at[0:12])
        sums = jnp.concatenate([ps_all[0], ps_all[1]], axis=1)
        up_half, down_half = sums[0:48], sums[48:96]
        grad_down = nn(up_half, normed[...])
        grad_query = nn(down_half[0:RANK], qall[i])
        grad_kv = [
            nt(down_half[(1 + p) * RANK : (2 + p) * RANK], kvg[p, mine, :]) for p in range(2)
        ]
        for d in range(8):
            for p in range(3):
                pay[8 * d + 2 * p : 8 * d + 2 * p + 2, :] = grad_down[
                    p * RANK + 2 * d : p * RANK + 2 * d + 2
                ]
            pay[8 * d + 6 : 8 * d + 8, 0:QC] = grad_query[2 * d : 2 * d + 2]
            for p in range(2):
                start = QC + p * 128
                pay[8 * d + 6 : 8 * d + 8, start : start + 16] = grad_kv[p][2 * d : 2 * d + 2]

        def send(k, _):
            to = (b + 1 + k) % ndp
            remote(
                pay.at[pl.ds(pl.multiple_of(8 * to, 8), 8), :], dp_in.at[b], dps, dpr, (to, i)
            ).start()
            return 0

        lax.fori_loop(0, ndp - 1, send, 0)
        dp_in[b] = pay[pl.ds(pl.multiple_of(8 * b, 8), 8), :]
        acc[...] += tn(up_half, adown[...].reshape(3 * RANK, NC))

    def step_dpout():
        for n in (11, 12, 13):
            loads[n].wait()
        if ndp > 1:
            drain(dp_in.at[0 : ndp - 1], dpr)
        total = dp_in[0]
        for n in range(1, ndp):
            total = total + dp_in[n]
        tokens = float(ndp * T)
        for p in range(3):
            out_d[p] = accd[p] + total[2 * p : 2 * p + 2, :] / tokens
        out_q[...] = accq[...] + ADAPTER_SCALE * total[6:8, 0:QC] / tokens
        for p in range(2):
            start = QC + p * 128
            out_kv[p] = acckv[p] + ADAPTER_SCALE * total[6:8, start : start + 16] / tokens

    def step_kv(p):
        def far_kv(k, _):
            wait_g(p, 2 * k + 1 - core)
            return 0

        lax.fori_loop(0, HALF, far_kv, 0)
        acc[...] += lax.dot_general(
            kvg[p], wkv[p], (((0,), (1,)), ((), ())), preferred_element_type=F32
        )

    def step_w():
        drain(wq, wsem)
        for n in (14, 15):
            loads[n].wait()

    steps = {
        "first": step_first, "col": step_col, "spr": step_spr, "fwd": step_fwd,
        "gfirst": step_gfirst, "gcol": step_gcol, "gfwd": step_gfwd, "mm": step_mm, "up": step_up, "up2": step_up2,
        "rsy": step_rsy, "rsz": step_rsz, "dp": step_dp, "dpout": step_dpout, "kv": step_kv,
        "w": step_w,
    }
    for name, *rest in ORDER:
        steps[name](*rest)
    out_i[0] = acc[...].astype(BF16)

    for n in range(3):
        by(own_in, kvs.at[n], kt.at[0:240, early], kt.at[:, early])
    for n, lanes in enumerate((late, slice(None))):
        ref = (vt, ut)[n]
        by(own_in, zs.at[n], ref.at[0:48, lanes], ref.at[0:64, lanes])

        @pl.when(own_in)
        def _():
            drain(qall.at[0, 0:192, :], ys.at[n])

    for p in range(2):
        by(own_in, rys.at[p], rs_src.at[p, 0], rs_src.at[p])

        @pl.when(own_in)
        def _():
            drain(rsz.at[p, 0:112, :], rzs.at[p])

        drain(kvg.at[p, 0:240, :], gs.at[p])
        drain(kvg.at[p, 0:256, :], gs.at[2 + p])
    for n, (first, last, _) in enumerate(CHUNKS):
        drain(qall.at[0:15, pl.ds(first, last - first), :], qs.at[n])
    drain(qall.at[0:16], fs)
    by(owner, pss, ps_in.at[0:11], ps_in.at[0:12])

    @pl.when(owner)
    def _():
        drain(ps_in.at[0 : NT - 1], pas)

    if ndp > 1:
        drain(dp_in.at[0 : ndp - 1], dps)


def hand_over(*refs):
    copies = [
        pltpu.make_async_copy(refs[n], refs[4 + n], refs[8].at[n]) for n in range(4)
    ]
    for copy in copies:
        copy.start()
    for copy in copies:
        copy.wait()


def per_device(
    ndp, normed, queries, keys, values, context_grad, segments, w_query, w_key, w_value,
    adapter_down, up_query, up_keyvalue, accum_down, accum_query, accum_keyvalue,
):
    tab, tabt = rotary_tables()
    keys_t = jnp.transpose(keys[0])
    values_t = jnp.transpose(values[0])
    vmem = pltpu.VMEM
    dma = pltpu.SemaphoreType.DMA
    scratch = [
        vmem((T, NC), BF16),
        vmem((T, QC), BF16),
        vmem((T, QC), BF16),
        vmem((1, T), jnp.int32),
        vmem((NT, NC, QC), BF16),
        vmem((2, NC, 512), BF16),
        vmem((3, RANK, NC), BF16),
        vmem((RANK, QC), BF16),
        vmem((2, RANK, 16), BF16),
        vmem(accum_down.shape, F32),
        vmem(accum_query.shape, F32),
        vmem(accum_keyvalue.shape, F32),
        vmem(tab.shape, F32),
        vmem(tabt.shape, F32),
        vmem((2, 16, T), BF16),
        vmem((2 * HD, T), BF16),
        vmem((2 * HD, T), BF16),
        vmem((16, 128), BF16),
        vmem((2 * HD, 128), BF16),
        vmem((2, 2, HD, T), BF16),
        vmem((2, NY, HD, T), BF16),
        vmem((2, HD, T), BF16),
        vmem((2, NZ, 16, T), BF16),
        vmem((NT, T, QC), BF16),
        vmem((2, 512, T), BF16),
        vmem((2, 96, 128), BF16),
        vmem((NT, 16, 128), BF16),
        vmem((2, 96, 128), BF16),
        vmem((64, NC), F32),
        vmem((8, 8, NC), F32),
        vmem((T, NC), F32),
        vmem((T, T), F32),
        dma((16,)), dma,
        dma((3,)), dma((3,)), dma((2,)), dma((2,)), dma((2,)), dma((2,)),
        dma((2,)), dma((2,)), dma((2,)), dma((2,)),
        dma((len(CHUNKS),)), dma((len(CHUNKS), NT)), dma, dma((NT,)), dma((4,)), dma((2, NT)),
        dma, dma, dma, dma, dma, dma,
    ]
    out_shape = (
        jax.ShapeDtypeStruct((1, T, NC), BF16),
        jax.ShapeDtypeStruct(accum_down.shape, F32),
        jax.ShapeDtypeStruct(accum_query.shape, F32),
        jax.ShapeDtypeStruct(accum_keyvalue.shape, F32),
    )
    results = pl.pallas_call(
        functools.partial(kernel, ndp),
        out_shape=tuple(pltpu.VMEM(o.shape, o.dtype) for o in out_shape),
        in_specs=[pl.BlockSpec(memory_space=pl.ANY)] * 17,
        out_specs=tuple(pl.BlockSpec(memory_space=pltpu.VMEM) for _ in out_shape),
        scratch_shapes=scratch,
        compiler_params=pltpu.CompilerParams(
            collective_id=0, has_side_effects=True, vmem_limit_bytes=63 * 1024 * 1024
        ),
    )(
        normed, queries, keys_t, values_t, context_grad, segments, w_query, w_key, w_value,
        adapter_down, up_query, up_keyvalue, accum_down, accum_query, accum_keyvalue,
        jnp.asarray(tab), jnp.asarray(tabt),
    )
    return pl.pallas_call(
        hand_over,
        out_shape=out_shape,
        in_specs=[pl.BlockSpec(memory_space=pltpu.VMEM)] * 4,
        out_specs=tuple(pl.BlockSpec(memory_space=pl.ANY) for _ in out_shape),
        scratch_shapes=[dma((4,))],
        compiler_params=pltpu.CompilerParams(vmem_limit_bytes=512 * 1024),
    )(*results)


def solution(mesh):
    in_specs = (
        P("dp", None, "tensor"),
        P("dp", None, "tensor"),
        P("dp", None, "tensor"),
        P("dp", None, "tensor"),
        P("dp", None, "tensor"),
        P("dp", None),
        P("tensor", None),
        P("tensor", None),
        P("tensor", None),
        P(None, None, "tensor"),
        P(None, "tensor"),
        P(None, None, "tensor"),
        P(None, "dp", "tensor"),
        P("dp", "tensor"),
        P(None, "dp", "tensor"),
    )
    out_specs = (
        P("dp", None, "tensor"),
        P(None, "dp", "tensor"),
        P("dp", "tensor"),
        P(None, "dp", "tensor"),
    )
    return jax.shard_map(
        functools.partial(per_device, mesh.shape["dp"]),
        mesh=mesh, in_specs=in_specs, out_specs=out_specs, check_vma=False,
    )
```

```python
import functools
import math

import jax
import jax.numpy as jnp
import numpy as np
from jax import lax
from jax.experimental import pallas as pl
from jax.experimental.pallas import tpu as pltpu
from jax.sharding import PartitionSpec as P

HD = 128
RANK = 16
ADAPTER_SCALE = 2.0
ROPE_BASE = 500000.0
F32 = jnp.float32
BF16 = jnp.bfloat16
MESH = pl.DeviceIdType.MESH

NY, NZ = 4, 4
NT = NY * NZ * 2
HALF = NT // 2
T = 256
QC = 256
NC = 512


def rotary_tables():
    exponent = np.arange(HD // 2, dtype=np.float32) * np.float32(2.0 / HD)
    frequency = (1.0 / np.float32(ROPE_BASE) ** exponent).astype(np.float32)
    wavelength = (2.0 * math.pi / frequency).astype(np.float32)
    blend = (8192.0 / wavelength - 1.0) / 3.0
    middle = (1.0 - blend) * frequency / 8.0 + blend * frequency
    scaled = np.where(
        wavelength < 2048.0, frequency, np.where(wavelength > 8192.0, frequency / 8.0, middle)
    ).astype(np.float32)
    angle = np.arange(T, dtype=np.float32)[:, None] * scaled[None, :]
    cosine = np.cos(angle).astype(np.float32)
    sine = np.sin(angle).astype(np.float32)
    rows = np.stack(
        [np.concatenate([cosine, cosine], 1), np.concatenate([sine, -sine], 1)]
    )
    cols = np.stack([cosine.T, sine.T])
    return rows, cols


def nt(left, right):
    return lax.dot_general(left, right, (((1,), (1,)), ((), ())), preferred_element_type=F32)


def nn(left, right):
    return lax.dot_general(left, right, (((1,), (0,)), ((), ())), preferred_element_type=F32)


def tn(left, right):
    return lax.dot_general(left, right, (((0,), (0,)), ((), ())), preferred_element_type=F32)


CHUNKS = ((0, 128, 'z'), (128, 224, 'z'), (224, 256, 'y'))

FAR = (
    (2, 2), (2, 1), (2, -1), (1, 2), (-1, 2), (0, 2), (1, 1), (1, -1), (-1, 1), (-1, -1),
    (2, 0), (0, 1), (0, -1), (1, 0), (-1, 0), (0, 0),
)

ORDER = (('up',), ('fwd', 0, 0, 0), ('fwd', 1, 0, 0), ('fwd', 2, 0, 0), ('w',), ('mm', 0, 0), ('spr', 0, 0, 1), ('spr', 0, 0, -1), ('fwd', 0, 1, 0), ('fwd', 0, -1, 0), ('col', 0, 1), ('col', 0, -1), ('fwd', 0, 0, 1), ('fwd', 0, 0, -1), ('rsy', 1), ('col', 1, 1), ('col', 1, -1), ('fwd', 1, 0, 1), ('fwd', 1, 0, -1), ('rsy', 0), ('spr', 1, 0, 1), ('spr', 1, 0, -1), ('spr', 2, 0, 1), ('spr', 2, 0, -1), ('fwd', 1, 1, 0), ('fwd', 1, -1, 0), ('fwd', 2, 0, 1), ('fwd', 2, 0, -1), ('col', 2, 1), ('col', 2, -1), ('fwd', 2, 1, 0), ('fwd', 2, -1, 0), ('mm', 0, 1), ('mm', 1, 0), ('mm', -1, 0), ('fwd', 0, 2, 0), ('mm', 0, -1), ('col', 0, 2), ('fwd', 0, 0, 2), ('spr', 0, 1, 1), ('spr', 0, 1, -1), ('fwd', 0, 1, 1), ('fwd', 0, -1, 1), ('up2',), ('col', 1, 2), ('fwd', 1, 0, 2), ('spr', 0, -1, 1), ('spr', 0, -1, -1), ('fwd', 0, 1, -1), ('fwd', 0, -1, -1), ('rsz', 1), ('gfirst', 1), ('fwd', 2, 0, 2), ('spr', 1, 1, 1), ('spr', 1, 1, -1), ('fwd', 1, 1, 1), ('fwd', 1, -1, 1), ('spr', 2, 1, 1), ('spr', 2, 1, -1), ('fwd', 2, 1, 1), ('fwd', 2, 1, -1), ('mm', 0, 2), ('rsz', 0), ('gfirst', 0), ('spr', 1, -1, 1), ('spr', 1, -1, -1), ('spr', 2, -1, 1), ('spr', 2, -1, -1), ('fwd', 2, -1, 1), ('fwd', 1, 1, -1), ('fwd', 1, -1, -1), ('fwd', 1, 2, 0), ('fwd', 2, -1, -1), ('mm', 1, 1), ('col', 2, 2), ('fwd', 2, 2, 0), ('mm', -1, 1), ('mm', 1, -1), ('mm', -1, -1), ('mm', 2, 0), ('gcol', 1, 1), ('spr', 0, 2, 1), ('spr', 0, 2, -1), ('gcol', 1, -1), ('fwd', 0, 1, 2), ('fwd', 0, -1, 2), ('fwd', 2, 1, 2), ('fwd', 0, 2, 1), ('gcol', 0, 1), ('gcol', 0, -1), ('fwd', 2, -1, 2), ('gcol', 1, 2), ('spr', 2, 2, 1), ('spr', 2, 2, -1), ('fwd', 2, 2, 1), ('fwd', 2, 2, -1), ('spr', 1, 2, 1), ('spr', 1, 2, -1), ('fwd', 1, 1, 2), ('fwd', 1, -1, 2), ('gcol', 0, 2), ('fwd', 0, 2, -1), ('mm', 1, 2), ('mm', -1, 2), ('fwd', 1, 2, 1), ('dp',), ('gfwd', 1, 0), ('fwd', 1, 2, -1), ('fwd', 2, 2, 2), ('mm', 2, 1), ('gfwd', 0, 0), ('fwd', 0, 2, 2), ('mm', 2, -1), ('gfwd', 1, 1), ('gfwd', 1, -1), ('fwd', 1, 2, 2), ('gfwd', 0, 1), ('gfwd', 0, -1), ('gfwd', 1, 2), ('mm', 2, 2), ('gfwd', 0, 2), ('kv', 1), ('kv', 0), ('dpout',))


def kernel(
    ndp,
    normed_h, queries_h, keys_h, values_h, cot_h, seg_h, wq_h, wk_h, wv_h,
    adown_h, upq_h, upkv_h, accd_h, accq_h, acckv_h, tab_h, tabt_h,
    out_i, out_d, out_q, out_kv,
    normed, queries, cot, seg, wq, wkv, adown, upq, upkv, accd, accq, acckv, tab, tabt,
    kvown, kt, vt, utown, ut, rs_src, rsy, rsz, rs_dst, qall, kvg, ps_src, ps_in, ps_all,
    pay, dp_in, acc, bias,
    lsem, wsem, kvs, kvr, zs, zr, ys, yr, rys, ryr, rzs, rzr, qs, qr, fs, fr, gs, gr,
    pss, psr, pas, par, dps, dpr,
):
    i = lax.axis_index("tensor")
    b = lax.axis_index("dp")
    core = lax.rem(i, 2)
    z = lax.rem(i // 2, NZ)
    y = i // (2 * NZ)
    side = i // HALF
    own_in = core == side

    rows_at = [lax.rem(y + d, NY) * (2 * NZ) for d in range(NY)]
    cols_at = [lax.rem(z + d, NZ) * 2 for d in range(NZ)]
    chip_at = [[r + c for c in cols_at] for r in rows_at]
    cores = (core, 1 - core)

    def dev(dy, dz, dc):
        return chip_at[dy % NY][dz % NZ] + cores[dc]

    def dev_side(dy, dz):
        return chip_at[dy % NY][dz % NZ] + side

    loads = [
        (keys_h, kvown.at[0]), (values_h, kvown.at[1]), (queries_h.at[0], queries),
        (cot_h.at[0], cot), (seg_h, seg), (normed_h.at[0], normed), (adown_h, adown),
        (upq_h, upq), (upkv_h, upkv), (tab_h, tab), (tabt_h, tabt),
        (accd_h, accd), (accq_h, accq), (acckv_h, acckv), (wk_h, wkv.at[0]), (wv_h, wkv.at[1]),
    ]
    loads = [pltpu.make_async_copy(src, dst, lsem.at[n]) for n, (src, dst) in enumerate(loads)]
    barrier = pltpu.get_barrier_semaphore()

    def greet(to):
        pl.semaphore_signal(barrier, 1, device_id=to, device_id_type=MESH)

    def greet_d(k, _):
        greet(((b + 1 + k) % ndp, i))
        return 0

    for copy in loads[:2]:
        copy.start()
    for n, (dy, dz) in enumerate(FAR):
        for dc in (1, 0):
            if (dy, dz, dc) != (0, 0, 0):
                greet((b, dev(dy, dz, dc)))
        if n == 6:
            lax.fori_loop(0, ndp - 1, greet_d, 0)
    for copy in loads[2:]:
        copy.start()

    def load_w(k, _):
        pltpu.make_async_copy(
            wq_h.at[:, pl.ds(pl.multiple_of(k * QC, QC), QC)], wq.at[k], wsem
        ).start()
        return 0

    def remote(src, dst, send, recv, to):
        return pltpu.make_async_remote_copy(
            src_ref=src, dst_ref=dst, send_sem=send, recv_sem=recv,
            device_id=to, device_id_type=MESH,
        )

    def drain(ref, sem):
        pltpu.make_async_copy(ref, ref, sem).wait()

    def by(test, sem, part, whole):
        @pl.when(test)
        def _():
            drain(part, sem)

        @pl.when(jnp.logical_not(test))
        def _():
            drain(whole, sem)

    owner = (i < 24) & (core == (i // 2) % 2)

    def piece(ref, n):
        return ref.at[n % 2, pl.ds(pl.multiple_of(16 * (n // 2), 16), 16), :]

    def scatter_sums():
        def send(k, _):
            n = (k % 3) * NZ + (z + 2 + k // 3) % NZ
            to = 2 * n + n % 2

            @pl.when(to != i)
            def _():
                remote(piece(ps_src, n), ps_in.at[i], pss, psr, (b, to)).start()

            return 0

        lax.fori_loop(0, 12, send, 0)

    def reduce_sums():
        @pl.when(owner)
        def _():
            n = i // 2
            rows = pl.ds(pl.multiple_of(16 * (n // 2), 16), 16)
            ps_in[i] = ps_src[n % 2, rows, :]
            drain(ps_in.at[0 : NT - 1], psr)
            ps_all[n % 2, rows, :] = jnp.sum(ps_in[...].astype(F32), axis=0).astype(BF16)

            def send(k, _):
                ref = piece(ps_all, n)
                remote(ref, ref, pas, par, (b, (i + 1 + k) % NT)).start()
                return 0

            lax.fori_loop(0, NT - 1, send, 0)

    loads[0].wait()
    loads[1].wait()
    pl.semaphore_wait(barrier, NT - 1 + ndp - 1)

    home = pl.ds(pl.multiple_of((i % HALF) * 16, 16), 16)

    def scatter_home(src, dst, send, recv, lanes=slice(None)):
        for dy, dz in FAR:
            to = dev_side(dy, dz)

            def start():
                remote(
                    src.at[:, lanes], dst.at[home, lanes], send, recv, (b, to)
                ).start()

            if (dy, dz) == (0, 0):
                pl.when(to != i)(start)
            else:
                start()

        @pl.when(own_in)
        def _():
            dst[home, lanes] = src[:, lanes]

    my_row = pl.ds(pl.multiple_of((y % 2) * HD, HD), HD)

    def along_z(src, dst, n, lanes):
        for dz in (2, 1, -1, 0):
            to = dev_side(0, dz)

            def start():
                remote(
                    src.at[:, lanes], dst.at[home, lanes], zs.at[n], zr.at[n], (b, to)
                ).start()

            if dz == 0:
                pl.when(to != i)(start)
            else:
                start()

        @pl.when(own_in)
        def _():
            dst[home, lanes] = src[:, lanes]

    def along_y(dst, n, lanes):
        @pl.when(own_in)
        def _():
            drain(dst.at[0:112, lanes], zr.at[n])
            for dy in (2, 1, -1):
                ref = dst.at[my_row, lanes]
                remote(ref, ref, ys.at[n], yr.at[n], (b, dev(dy, 0, 0))).start()

    early, late = slice(0, T // 2), slice(T // 2, T)
    scatter_home(kvown.at[0], kt, kvs.at[0], kvr.at[0], early)
    scatter_home(kvown.at[1], vt, kvs.at[1], kvr.at[1], early)
    scatter_home(kvown.at[0], kt, kvs.at[2], kvr.at[2], late)
    scatter_home(kvown.at[1], vt, kvs.at[3], kvr.at[3], late)
    loads[8].wait()
    rank = lax.broadcasted_iota(jnp.int32, (RANK, 128), 0)
    lane = lax.broadcasted_iota(jnp.int32, (RANK, 128), 1)
    columns = jnp.zeros((16, 128), F32)
    for p in range(2):
        place = jnp.where(lane == rank + p * RANK, 1.0, 0.0).astype(BF16)
        columns = columns + tn(upkv[p], place)
    utown[...] = columns.astype(BF16)
    along_z(utown, ut, 1, slice(None))

    loads[5].wait()
    loads[6].wait()
    down_part = nt(adown[...].reshape(3 * RANK, NC), normed[...]).astype(BF16)
    for n in range(2):
        ps_src[n, 48:96, :] = down_part[:, n * 128 : (n + 1) * 128]
    loads[4].wait()
    doc = jnp.broadcast_to(seg[...].astype(F32), (T, T))
    row = lax.broadcasted_iota(jnp.int32, (T, T), 0)
    col = lax.broadcasted_iota(jnp.int32, (T, T), 1)
    bias[...] = jnp.where((col <= row) & (doc == doc.T), 0.0, -jnp.inf)
    acc[...] = jnp.zeros_like(acc)
    for n in (2, 3, 7, 9, 10):
        loads[n].wait()

    class Gather:
        def __init__(self, axis, ref, send, recv):
            self.axis, self.ref, self.s, self.r = axis, ref, send, recv

        def at(self, d, e):
            return dev(e, d, 0) if self.axis == "z" else dev(d, e, 0)

        def push(self, slot, to, part=None):
            ref = self.ref(slot, part)
            remote(ref, ref, self.s, self.r.at[slot], (b, to)).start()

        def wait(self, slot):
            drain(self.ref(slot, None), self.r.at[slot])

        def first(self):
            for d, e in ((1, 0), (-1, 0), (0, 1), (0, -1)):
                self.push(i, self.at(d, e))

        def col(self, d):
            slot = self.at(d, 0)
            self.wait(slot)
            if d != 2:
                self.push(slot, self.at(-d, 0), 0 if d == -1 else 1)
            for e in (1, -1):
                self.push(slot, self.at(0, e))

        def spr(self, d, e):
            slot = self.at(d, e)
            self.wait(slot)
            self.push(slot, self.at(0, -e), 0 if e == -1 else 1)

        def far(self, dy, dz):
            if (dy if self.axis == "z" else dz) == 2:
                self.wait(dev(dy, dz, 0))

    def q_ref(first, last):
        half = (last - first) // 2

        def ref(slot, part):
            if part is None:
                return qall.at[slot, pl.ds(first, last - first), :]
            return qall.at[slot, pl.ds(first + part * half, half), :]

        return ref

    def g_ref(p, slot):
        return kvg.at[p, pl.ds(pl.multiple_of(slot * 16, 16), 16), :]

    gathers = {
        n: Gather(axis, q_ref(first, last), qs.at[n], qr.at[n])
        for n, (first, last, axis) in enumerate(CHUNKS)
    }
    mine = pl.ds(pl.multiple_of(i * 16, 16), 16)
    other = i + 1 - 2 * core

    def send_rsy(p, h):
        to = ((2 * core + h) * NZ + z) * 2 + core

        @pl.when(to != i)
        def _():
            remote(rs_src.at[p, h], rsy.at[p, y], rys.at[p], ryr.at[p], (b, to)).start()

        @pl.when(to == i)
        def _():
            rsy[p, y] = rs_src[p, h]

    def wait_home(n, ref, lanes):
        by(own_in, kvr.at[n], ref.at[0:240, lanes], ref.at[:, lanes])

    scale = 1.0 / math.sqrt(HD)
    heads = [slice(0, HD), slice(HD, 2 * HD)]
    cosine, sine = tabt[0], tabt[1]

    def softmax(h, rows, keys):
        scores = nn(queries[rows, h], kt[h, keys]) * scale + bias[rows, keys]
        weights = jnp.exp(scores - jnp.max(scores, axis=1, keepdims=True))
        return weights / jnp.sum(weights, axis=1, keepdims=True)

    def score_cotangent(h, rows, keys, weights):
        weight_grad = nn(cot[rows, h], vt[h, keys])
        delta = jnp.sum(weights * weight_grad, axis=1, keepdims=True)
        return (weights * (weight_grad - delta)).astype(BF16)

    def query_cotangent(h, rows, keys, score_grad):
        rot = nt(score_grad, kt[h, keys]) * scale
        qall[i, rows, h] = (
            rot * tab[0, rows, :] + pltpu.roll(rot, HD // 2, 1) * tab[1, rows, :]
        ).astype(BF16)

    def both(left, one, two):
        top = tn(left[early], one)
        rest = tn(left[late], two)
        return jnp.concatenate([rest[:, early] + top, rest[:, late]], axis=1)

    every = slice(0, T)
    wait_home(0, kt, early)
    probs_early = [softmax(h, early, early) for h in heads]
    wait_home(1, vt, early)
    grads_early = []
    for n, h in enumerate(heads):
        grads_early.append(score_cotangent(h, early, early, probs_early[n]))
        query_cotangent(h, early, early, grads_early[n])
    gathers[0].first()
    along_y(ut, 1, slice(None))
    wait_home(2, kt, late)
    probs = []
    for n, h in enumerate(heads):
        probs.append(softmax(h, late, every))
        rs_src[1, n] = both(
            cot[:, h], probs_early[n].astype(BF16), probs[n].astype(BF16)
        ).astype(BF16)
        send_rsy(1, n)
    wait_home(3, vt, late)
    grads = []
    for n, h in enumerate(heads):
        grads.append(score_cotangent(h, late, every, probs[n]))
        query_cotangent(h, late, every, grads[n])
    for n in range(1, len(CHUNKS)):
        gathers[n].first()
    for n, h in enumerate(heads):
        key_rot = both(queries[:, h], grads_early[n], grads[n]) * scale
        one, two = key_rot[: HD // 2], key_rot[HD // 2 :]
        rs_src[0, n] = jnp.concatenate(
            [one * cosine + two * sine, two * cosine - one * sine], axis=0
        ).astype(BF16)
        send_rsy(0, n)
    lax.fori_loop(0, NT, load_w, 0)

    def step_first(tag):
        gathers[tag].first()

    def step_col(tag, d):
        gathers[tag].col(d)

    def step_spr(tag, d, e):
        gathers[tag].spr(d, e)

    def step_fwd(n, dy, dz):
        gathers[n].far(dy, dz)
        slot = dev(dy, dz, 0)
        ref = gathers[n].ref(slot, None)
        remote(ref, ref, fs, fr.at[slot], (b, other)).start()

    def push_g(p, slot, to):
        ref = g_ref(p, slot)
        remote(ref, ref, gs.at[p], gr.at[p, slot], (b, to)).start()

    def wait_g(p, slot):
        drain(g_ref(p, slot), gr.at[p, slot])

    def step_gfirst(p):
        for dy, dz in ((0, 2), (0, 1), (0, -1), (2, 0), (1, 0), (-1, 0)):
            push_g(p, i, dev(dy, dz, 0))

    def step_gcol(p, dz):
        wait_g(p, dev(0, dz, 0))
        for dy in (2, 1, -1):
            push_g(p, dev(0, dz, 0), dev(dy, 0, 0))

    def step_gfwd(p, dz):
        for dy in (0, 1, -1, 2):
            slot = dev(dy, dz, 0)
            if dy != 0:
                wait_g(p, slot)
            ref = g_ref(p, slot)
            remote(ref, ref, gs.at[2 + p], gr.at[p, slot], (b, other)).start()

    def step_mm(dy, dz):
        one, two = dev(dy, dz, 0), dev(dy, dz, 1)
        drain(qall.at[two], fr.at[two])
        acc[...] += nt(qall[one], wq[one]) + nt(qall[two], wq[two])

    def step_up():
        by(own_in, yr.at[1], ut.at[0:HD, :], ut)
        sums = [nt(upq[...], qall[i])]
        for p in range(2):
            part = rs_src[p].reshape(2 * HD, T)
            sums.append(tn(ut[...], part)[p * RANK : (p + 1) * RANK])
        up_part = (ADAPTER_SCALE * jnp.concatenate(sums, axis=0)).astype(BF16)
        for n in range(2):
            ps_src[n, 0:48, :] = up_part[:, n * 128 : (n + 1) * 128]
        scatter_sums()

    def step_up2():
        reduce_sums()

    def step_rsy(p):
        @pl.when(own_in)
        def _():
            drain(rsy.at[p, 0 : NY - 1], ryr.at[p])
            total = rsy[p, 0].astype(F32)
            for n in range(1, NY):
                total = total + rsy[p, n].astype(F32)
            rsz[p] = total.astype(BF16)
            for dz in (2, 1, -1, 0):
                for dc in range(2):
                    to = dev(0, dz, dc)
                    rows = pl.ds(pl.multiple_of(16 * (to % (2 * NZ)), 16), 16)
                    if (dz, dc) == (0, 0):
                        rs_dst[p, z] = rsz[p, rows, :]
                    else:
                        remote(
                            rsz.at[p, rows, :], rs_dst.at[p, z], rzs.at[p], rzr.at[p], (b, to)
                        ).start()

    def step_rsz(p):
        by(own_in, rzr.at[p], rs_dst.at[p, 0 : NZ - 1], rs_dst.at[p])
        total = rs_dst[p, 0].astype(F32)
        for n in range(1, NZ):
            total = total + rs_dst[p, n].astype(F32)
        kvg[p, mine, :] = total.astype(BF16)

    def step_dp():
        by(owner, par, ps_in.at[0:11], ps_in.at[0:12])
        sums = jnp.concatenate([ps_all[0], ps_all[1]], axis=1)
        up_half, down_half = sums[0:48], sums[48:96]
        grad_down = nn(up_half, normed[...])
        grad_query = nn(down_half[0:RANK], qall[i])
        grad_kv = [
            nt(down_half[(1 + p) * RANK : (2 + p) * RANK], kvg[p, mine, :]) for p in range(2)
        ]
        for d in range(8):
            for p in range(3):
                pay[8 * d + 2 * p : 8 * d + 2 * p + 2, :] = grad_down[
                    p * RANK + 2 * d : p * RANK + 2 * d + 2
                ]
            pay[8 * d + 6 : 8 * d + 8, 0:QC] = grad_query[2 * d : 2 * d + 2]
            for p in range(2):
                start = QC + p * 128
                pay[8 * d + 6 : 8 * d + 8, start : start + 16] = grad_kv[p][2 * d : 2 * d + 2]

        def send(k, _):
            to = (b + 1 + k) % ndp
            remote(
                pay.at[pl.ds(pl.multiple_of(8 * to, 8), 8), :], dp_in.at[b], dps, dpr, (to, i)
            ).start()
            return 0

        lax.fori_loop(0, ndp - 1, send, 0)
        dp_in[b] = pay[pl.ds(pl.multiple_of(8 * b, 8), 8), :]
        acc[...] += tn(up_half, adown[...].reshape(3 * RANK, NC))

    def step_dpout():
        for n in (11, 12, 13):
            loads[n].wait()
        if ndp > 1:
            drain(dp_in.at[0 : ndp - 1], dpr)
        total = dp_in[0]
        for n in range(1, ndp):
            total = total + dp_in[n]
        tokens = float(ndp * T)
        for p in range(3):
            out_d[p] = accd[p] + total[2 * p : 2 * p + 2, :] / tokens
        out_q[...] = accq[...] + ADAPTER_SCALE * total[6:8, 0:QC] / tokens
        for p in range(2):
            start = QC + p * 128
            out_kv[p] = acckv[p] + ADAPTER_SCALE * total[6:8, start : start + 16] / tokens

    def step_kv(p):
        def far_kv(k, _):
            wait_g(p, 2 * k + 1 - core)
            return 0

        lax.fori_loop(0, HALF, far_kv, 0)
        acc[...] += lax.dot_general(
            kvg[p], wkv[p], (((0,), (1,)), ((), ())), preferred_element_type=F32
        )

    def step_w():
        drain(wq, wsem)
        for n in (14, 15):
            loads[n].wait()

    steps = {
        "first": step_first, "col": step_col, "spr": step_spr, "fwd": step_fwd,
        "gfirst": step_gfirst, "gcol": step_gcol, "gfwd": step_gfwd, "mm": step_mm, "up": step_up, "up2": step_up2,
        "rsy": step_rsy, "rsz": step_rsz, "dp": step_dp, "dpout": step_dpout, "kv": step_kv,
        "w": step_w,
    }
    for name, *rest in ORDER:
        steps[name](*rest)
    out_i[0] = acc[...].astype(BF16)

    for n in range(4):
        by(own_in, kvs.at[n], kt.at[0:240, early], kt.at[:, early])
    for n, lanes, ref in ((1, slice(None), ut),):
        by(own_in, zs.at[n], ref.at[0:48, lanes], ref.at[0:64, lanes])

        @pl.when(own_in)
        def _():
            drain(qall.at[0, 0:192, :], ys.at[n])

    for p in range(2):
        by(own_in, rys.at[p], rs_src.at[p, 0], rs_src.at[p])

        @pl.when(own_in)
        def _():
            drain(rsz.at[p, 0:112, :], rzs.at[p])

        drain(kvg.at[p, 0:240, :], gs.at[p])
        drain(kvg.at[p, 0:256, :], gs.at[2 + p])
    for n, (first, last, _) in enumerate(CHUNKS):
        drain(qall.at[0:15, pl.ds(first, last - first), :], qs.at[n])
    drain(qall.at[0:16], fs)
    by(owner, pss, ps_in.at[0:11], ps_in.at[0:12])

    @pl.when(owner)
    def _():
        drain(ps_in.at[0 : NT - 1], pas)

    if ndp > 1:
        drain(dp_in.at[0 : ndp - 1], dps)


def hand_over(*refs):
    copies = [
        pltpu.make_async_copy(refs[n], refs[4 + n], refs[8].at[n]) for n in range(4)
    ]
    for copy in copies:
        copy.start()
    for copy in copies:
        copy.wait()


def per_device(
    ndp, normed, queries, keys, values, context_grad, segments, w_query, w_key, w_value,
    adapter_down, up_query, up_keyvalue, accum_down, accum_query, accum_keyvalue,
):
    tab, tabt = rotary_tables()
    keys_t = jnp.transpose(keys[0])
    values_t = jnp.transpose(values[0])
    vmem = pltpu.VMEM
    dma = pltpu.SemaphoreType.DMA
    scratch = [
        vmem((T, NC), BF16),
        vmem((T, QC), BF16),
        vmem((T, QC), BF16),
        vmem((1, T), jnp.int32),
        vmem((NT, NC, QC), BF16),
        vmem((2, NC, 512), BF16),
        vmem((3, RANK, NC), BF16),
        vmem((RANK, QC), BF16),
        vmem((2, RANK, 16), BF16),
        vmem(accum_down.shape, F32),
        vmem(accum_query.shape, F32),
        vmem(accum_keyvalue.shape, F32),
        vmem(tab.shape, F32),
        vmem(tabt.shape, F32),
        vmem((2, 16, T), BF16),
        vmem((2 * HD, T), BF16),
        vmem((2 * HD, T), BF16),
        vmem((16, 128), BF16),
        vmem((2 * HD, 128), BF16),
        vmem((2, 2, HD, T), BF16),
        vmem((2, NY, HD, T), BF16),
        vmem((2, HD, T), BF16),
        vmem((2, NZ, 16, T), BF16),
        vmem((NT, T, QC), BF16),
        vmem((2, 512, T), BF16),
        vmem((2, 96, 128), BF16),
        vmem((NT, 16, 128), BF16),
        vmem((2, 96, 128), BF16),
        vmem((64, NC), F32),
        vmem((8, 8, NC), F32),
        vmem((T, NC), F32),
        vmem((T, T), F32),
        dma((16,)), dma,
        dma((4,)), dma((4,)), dma((2,)), dma((2,)), dma((2,)), dma((2,)),
        dma((2,)), dma((2,)), dma((2,)), dma((2,)),
        dma((len(CHUNKS),)), dma((len(CHUNKS), NT)), dma, dma((NT,)), dma((4,)), dma((2, NT)),
        dma, dma, dma, dma, dma, dma,
    ]
    out_shape = (
        jax.ShapeDtypeStruct((1, T, NC), BF16),
        jax.ShapeDtypeStruct(accum_down.shape, F32),
        jax.ShapeDtypeStruct(accum_query.shape, F32),
        jax.ShapeDtypeStruct(accum_keyvalue.shape, F32),
    )
    results = pl.pallas_call(
        functools.partial(kernel, ndp),
        out_shape=tuple(pltpu.VMEM(o.shape, o.dtype) for o in out_shape),
        in_specs=[pl.BlockSpec(memory_space=pl.ANY)] * 17,
        out_specs=tuple(pl.BlockSpec(memory_space=pltpu.VMEM) for _ in out_shape),
        scratch_shapes=scratch,
        compiler_params=pltpu.CompilerParams(
            collective_id=0, has_side_effects=True, vmem_limit_bytes=63 * 1024 * 1024
        ),
    )(
        normed, queries, keys_t, values_t, context_grad, segments, w_query, w_key, w_value,
        adapter_down, up_query, up_keyvalue, accum_down, accum_query, accum_keyvalue,
        jnp.asarray(tab), jnp.asarray(tabt),
    )
    return pl.pallas_call(
        hand_over,
        out_shape=out_shape,
        in_specs=[pl.BlockSpec(memory_space=pltpu.VMEM)] * 4,
        out_specs=tuple(pl.BlockSpec(memory_space=pl.ANY) for _ in out_shape),
        scratch_shapes=[dma((4,))],
        compiler_params=pltpu.CompilerParams(vmem_limit_bytes=512 * 1024),
    )(*results)


def solution(mesh):
    in_specs = (
        P("dp", None, "tensor"),
        P("dp", None, "tensor"),
        P("dp", None, "tensor"),
        P("dp", None, "tensor"),
        P("dp", None, "tensor"),
        P("dp", None),
        P("tensor", None),
        P("tensor", None),
        P("tensor", None),
        P(None, None, "tensor"),
        P(None, "tensor"),
        P(None, None, "tensor"),
        P(None, "dp", "tensor"),
        P("dp", "tensor"),
        P(None, "dp", "tensor"),
    )
    out_specs = (
        P("dp", None, "tensor"),
        P(None, "dp", "tensor"),
        P("dp", "tensor"),
        P(None, "dp", "tensor"),
    )
    return jax.shard_map(
        functools.partial(per_device, mesh.shape["dp"]),
        mesh=mesh, in_specs=in_specs, out_specs=out_specs, check_vma=False,
    )
```
